128 devices in a mesh: seq: 32 (over z, y, core), width: 4 (over x).
Axes of the slice: x: 4, y: 4, z: 4, core: 2. Of those that a mesh axis runs over, the one named last changes fastest.
Arguments:
- tokens: bfloat16 [32768, 4096], P('seq', 'width'), may hold values from -8 to 8
- slot_param: bfloat16 [4096, 1024], P('width'), may hold values from -10 to 10
- scale: float32 [1], replicated, may hold values from 250 to 400
- w_in: bfloat16 [8, 4096, 16384], P(None, 'width', 'seq'), may hold values from -0.09375 to 0.09375
- w_out: bfloat16 [8, 16384, 4096], P(None, 'seq', 'width'), may hold values from -0.046875 to 0.046875
Outputs:
- mixed: bfloat16 [32768, 4096], P('seq', 'width')
The draws below stay inside these ranges and needn't reach their ends.
All inputs are finite; a program needn't handle non-finite values.
Results may differ from the reference program's by a relative error of at most 0.012.
Values may be sent and summed in bfloat16 or wider, within the bound.
A program may use at most 128 MiB of HBM per device.

```python
import math
import jax
import jax.numpy as jnp
from jax import lax

D = 4096
FF = 16384
SLOT_PER = 16
E_RUN = 8
TOKENS = 32768
S_ALL = 1024
WINDOW = 128


def base_param(key):
    return jnp.clip(jax.random.normal(key, (D, S_ALL), jnp.float32), -4.5, 4.5)


def shared_scale(key):
    return jnp.exp(jax.random.uniform(jax.random.fold_in(key, 91), (1,), jnp.float32, math.log(250.0), math.log(400.0)))


def draw_scale(key, part):
    return shared_scale(key)


def draw_slot_param(key, part):
    shared = base_param(key)
    return shared.astype(jnp.bfloat16)


def draw_tokens(key, part):
    key = jax.random.fold_in(key, 2)
    values = jnp.clip(jax.random.normal(key, (TOKENS, D), jnp.float32), -4.5, 4.5)
    return values.astype(jnp.bfloat16)


def block_scale(stream_key, shape, cuts, low, top_value):
    def one(axis_at, blocks):
        heights = jax.random.uniform(jax.random.fold_in(jax.random.fold_in(stream_key, 6), axis_at), (blocks,), jnp.float32, low / len(cuts), top_value / len(cuts))
        return jnp.repeat(jnp.exp(heights), shape[axis_at] // blocks).reshape((-1,) + (1,) * (len(shape) - axis_at - 1))

    loudness = one(*cuts[0])
    for cut in cuts[1:]:
        loudness = loudness * one(*cut)
    return loudness


def noise(stream_key, extent, deviation, most, shards=(), kind=jnp.bfloat16):
    result = deviation * jax.random.normal(stream_key, extent, jnp.float32)
    if shards:
        result = result * block_scale(stream_key, extent, shards, -0.22, 0.18)
    return jnp.clip(result, -most, most).astype(kind)


def setup_inputs(seed: int = 0) -> dict:
    key_list = jax.random.split(jax.random.key(seed), 6)
    return {
        "tokens": draw_tokens(jax.random.fold_in(key_list[5], 71), 0),
        "slot_param": draw_slot_param(jax.random.fold_in(key_list[5], 71), 0),
        "scale": draw_scale(jax.random.fold_in(key_list[5], 71), 0),
        "w_in": noise(key_list[3], (E_RUN, D, FF), D ** -0.5, 0.09375, ((1, 4), (2, 32))),
        "w_out": noise(key_list[4], (E_RUN, FF, D), FF ** -0.5, 0.046875, ((1, 32), (2, 4))),
    }


EPS = 1e-06

def reference(tokens, slot_param, scale, w_in, w_out):
    raw = jnp.dot(tokens, slot_param, preferred_element_type=jnp.float32)
    token_float = tokens.astype(jnp.float32)
    row_squares = lax.optimization_barrier(jnp.sum(token_float * token_float, axis=1))
    param_float = slot_param.astype(jnp.float32)
    column_squares = lax.optimization_barrier(jnp.sum(param_float * param_float, axis=0))
    logits = scale[0] * raw / (jnp.sqrt(row_squares + EPS)[:, None] * jnp.sqrt(column_squares + EPS)[None, :])
    window_logits = logits[:, :WINDOW]
    slot_max = lax.optimization_barrier(jnp.max(window_logits, axis=0))
    dispatch = jnp.exp(window_logits - slot_max[None, :]).astype(jnp.bfloat16)
    slot_total = lax.optimization_barrier(jnp.sum(dispatch.astype(jnp.float32), axis=0))
    weighted = jnp.dot(dispatch.T, tokens, preferred_element_type=jnp.float32)
    slot_in = (weighted / slot_total[:, None]).astype(jnp.bfloat16)
    outputs = []
    for expert in range(E_RUN):
        rows = slot_in[expert * SLOT_PER:(expert + 1) * SLOT_PER]
        hidden_sum = jnp.dot(rows, w_in[expert], preferred_element_type=jnp.float32)
        hidden = jax.nn.gelu(hidden_sum, approximate=False).astype(jnp.bfloat16)
        outputs.append(jnp.dot(hidden, w_out[expert], preferred_element_type=jnp.float32))
    slot_out = jnp.concatenate(outputs, axis=0).astype(jnp.bfloat16)
    token_max = lax.optimization_barrier(jnp.max(logits, axis=1))
    token_total = lax.optimization_barrier(jnp.sum(jnp.exp(logits - token_max[:, None]), axis=1))
    combine = (jnp.exp(window_logits - token_max[:, None]) / token_total[:, None]).astype(jnp.bfloat16)
    return jnp.dot(combine, slot_out, preferred_element_type=jnp.float32).astype(jnp.bfloat16)
```

```python
import jax
import jax.numpy as jnp
from jax import lax
from jax.experimental import pallas as pl
from jax.experimental.pallas import tpu as pltpu
from jax.sharding import PartitionSpec as P

SLOT_PER = 16
E_RUN = 8
WINDOW = 128
EPS = 1e-06
F32 = jnp.float32
BF16 = jnp.bfloat16
MESH = pl.DeviceIdType.MESH
QT = 256
REST = 896
CHIPS = 16
SENDS = (2, 1, 3)
ARRIVALS = (0, 1, 3, 2)


def column(row):
    return jnp.transpose(jnp.broadcast_to(row, (128, 128)))


def kernel(
    tok_h, sp_h, scale_ref, win_h, wout_h,
    comb_o, so_o,
    tok, spw, spn, win, wout,
    wsend, wrecv, lw, rnv, dsp, nsend, nrecv,
    wb, pr, ab, rb, gs, si,
    hp, hr, hb, ob, po, ab2, ro, so, cb,
    ld_sem, x_send, x_recv, c_send, c_recv, s_send, s_recv, f_send, f_recv,
):
    s = lax.axis_index("seq")
    x = lax.axis_index("width")
    c = lax.rem(s, 2)
    p = lax.div(s, 2)
    z = lax.div(p, 4)
    y = lax.rem(p, 4)
    peer = (s + 1 - 2 * c, x)

    def xdev(d):
        return (s, lax.rem(x + d, 4))

    def chip_of(j):
        return lax.rem(z + j // 4, 4) * 4 + lax.rem(y + j % 4, 4)

    def chip_from(j):
        return lax.rem(z + 4 - j // 4, 4) * 4 + lax.rem(y + 4 - j % 4, 4)

    pending = []

    def remote(src, dst, send, recv, to):
        cp = pltpu.make_async_remote_copy(
            src_ref=src, dst_ref=dst, send_sem=send, recv_sem=recv, device_id=to, device_id_type=MESH
        )
        cp.start()
        pending.append(cp)
        return cp

    def load(src, dst, i):
        cp = pltpu.make_async_copy(src, dst, ld_sem.at[i])
        cp.start()
        return cp

    ld_spw = load(sp_h.at[:, pl.ds(0, WINDOW)], spw, 0)
    ld_tok = {}
    for i, d in enumerate((2, 1, 3, 0)):
        rows = pl.ds(lax.rem(x + d, 4) * QT, QT)
        ld_tok[d] = load(tok_h.at[rows], tok.at[rows], 1 + i)
    ld_spn = load(sp_h.at[:, pl.ds(WINDOW, REST)], spn, 5)
    ld_win = {}
    for i, d in enumerate((2, 1, 3, 0)):
        e = 2 * lax.rem(x + d, 4)
        ld_win[d] = load(win_h.at[pl.ds(e, 2)], win.at[pl.ds(e, 2)], 6 + i)
    ld_wout = {}
    for i, d in enumerate(ARRIVALS):
        e = 2 * lax.rem(x + 4 - d, 4)
        ld_wout[d] = load(wout_h.at[pl.ds(e, 2)], wout.at[pl.ds(e, 2)], 10 + i)

    barrier = pltpu.get_barrier_semaphore()
    for d in (1, 2, 3):
        pl.semaphore_signal(barrier, inc=1, device_id=xdev(d), device_id_type=MESH)
    pl.semaphore_signal(barrier, inc=1, device_id=peer, device_id_type=MESH)
    for j in range(1, CHIPS):
        pl.semaphore_signal(barrier, inc=1, device_id=(chip_of(j) * 2 + c, x), device_id_type=MESH)

    ld_spw.wait()
    spf = spw[...].astype(F32)
    csq = jnp.sum(spf * spf, axis=0, keepdims=True)
    xw = {}
    for d in (2, 1, 3, 0):
        ld_tok[d].wait()
        t = tok[pl.ds(lax.rem(x + d, 4) * QT, QT), :]
        wsend[d, 0:QT, :] = jnp.dot(t, spw[...], preferred_element_type=F32)
        part = jnp.zeros((QT, 128), F32)
        for b in range(8):
            tf = t[:, b * 128:(b + 1) * 128].astype(F32)
            part = part + tf * tf
        rows = [jnp.sum(jnp.transpose(part[h * 128:(h + 1) * 128]), axis=0, keepdims=True) for h in range(2)]
        wsend[d, QT:QT + 8, :] = jnp.concatenate(rows + [csq, jnp.zeros((5, 128), F32)], axis=0)
        if d == 2:
            pl.semaphore_wait(barrier, 19)
        if d:
            xw[d] = remote(wsend.at[d], wrecv.at[d], x_send.at[0, d], x_recv.at[0, d], xdev(d))
    tot = wsend[0]
    for d in (1, 3, 2):
        xw[d].wait_recv()
        tot = tot + wrecv[d]
    rn = jnp.sqrt(jnp.concatenate([column(tot[QT:QT + 1]), column(tot[QT + 1:QT + 2])], axis=0) + EPS)
    cn = jnp.sqrt(tot[QT + 2:QT + 3] + EPS)
    scale = scale_ref[0]
    logits = scale * tot[0:QT] / (rn * cn)
    lw[...] = logits
    rnv[...] = rn
    m = jnp.max(logits, axis=0, keepdims=True).astype(BF16)
    dsp[x, 0:QT, :] = jnp.exp(logits - m.astype(F32)).astype(BF16)
    dsp[x, QT:QT + 16, :] = jnp.broadcast_to(m, (16, 128))
    xd = {d: remote(dsp.at[x], dsp.at[x], x_send.at[1, d], x_recv.at[1, d], xdev(d)) for d in SENDS}

    ld_spn.wait()
    csn = jnp.zeros((8, REST), F32)
    for b in range(32):
        sf = spn[b * 32:(b + 1) * 32, :].astype(F32)
        sq = sf * sf
        csn = csn + sq[0:8] + sq[8:16] + sq[16:24] + sq[24:32]
    xn = {}
    for d in (2, 1, 3, 0):
        t = tok[pl.ds(lax.rem(x + d, 4) * QT, QT), :]
        nsend[d, 0:QT, :] = jnp.dot(t, spn[...], preferred_element_type=F32)
        nsend[d, QT:QT + 8, :] = csn
        if d:
            xn[d] = remote(nsend.at[d], nrecv.at[d], x_send.at[2, d], x_recv.at[2, d], xdev(d))

    for d in SENDS:
        xd[d].wait_recv()
    ms = [dsp[q, QT:QT + 1, :].astype(F32) for q in range(4)]
    mseq = jnp.maximum(jnp.maximum(ms[0], ms[1]), jnp.maximum(ms[2], ms[3]))
    total = jnp.zeros((1, 128), F32)
    cols = []
    for q in range(4):
        f = jnp.exp(ms[q] - mseq)
        total = total + f * jnp.sum(dsp[q, 0:QT, :].astype(F32), axis=0, keepdims=True)
        cols.append(column(f))
    stats = jnp.concatenate([mseq, total, jnp.zeros((6, 128), F32)], axis=0)
    for h in range(2):
        for k in range(2):
            at = h * 512 + k * 256
            acc = jnp.zeros((128, 256), F32)
            for q in range(4):
                prod = lax.dot_general(
                    dsp[q, 0:QT, :], tok[q * QT:(q + 1) * QT, at:at + 256],
                    (((0,), (0,)), ((), ())), preferred_element_type=F32,
                )
                acc = acc + prod * jnp.concatenate([cols[q], cols[q]], axis=1)
            for e in range(E_RUN):
                for b in range(2):
                    wb[k, e * 2 + h, b * 16:(b + 1) * 16, :] = acc[e * 16:(e + 1) * 16, b * 128:(b + 1) * 128]
                wb[k, e * 2 + h, 32:40, :] = stats

    cw = remote(wb.at[1 - c], pr, c_send.at[0], c_recv.at[0], peer)
    cw.wait_recv()
    m_a, m_b = wb[c, 0, 32:33, :], pr[0, 32:33, :]
    m2 = jnp.maximum(m_a, m_b)
    f_a, f_b = jnp.exp(m_a - m2), jnp.exp(m_b - m2)
    t2 = f_a * wb[c, 0, 33:34, :] + f_b * pr[0, 33:34, :]
    stats = jnp.concatenate([m2, t2, jnp.zeros((6, 128), F32)], axis=0)
    c_a, c_b = column(f_a), column(f_b)
    for i in range(CHIPS):
        e = i // 2
        k_a, k_b = c_a[e * 16:(e + 1) * 16], c_b[e * 16:(e + 1) * 16]
        for b in range(2):
            r = slice(b * 16, (b + 1) * 16)
            ab[i, r, :] = wb[c, i, r, :] * k_a + pr[i, r, :] * k_b
        ab[i, 32:40, :] = stats
    sw = {
        j: remote(ab.at[chip_of(j)], rb.at[j], s_send.at[0, j], s_recv.at[0, j], (chip_of(j) * 2 + c, x))
        for j in range(1, CHIPS)
    }
    for j in range(1, CHIPS):
        sw[j].wait_recv()
    mr = [ab[p, 32:33, :]] + [rb[j, 32:33, :] for j in range(1, CHIPS)]
    tr = [ab[p, 33:34, :]] + [rb[j, 33:34, :] for j in range(1, CHIPS)]
    top = mr[0]
    for v in mr[1:]:
        top = jnp.maximum(top, v)
    fr = [jnp.exp(v - top) for v in mr]
    total = fr[0] * tr[0]
    for f, t in zip(fr[1:], tr[1:]):
        total = total + f * t
    gs[...] = jnp.transpose(jnp.concatenate([f / total for f in fr] + [jnp.zeros((112, 128), F32)], axis=0))
    ge = gs[pl.ds(lax.div(p, 2) * 16, 16), :]
    acc = [jnp.zeros((16, 128), F32)] * 2
    for j in range(CHIPS):
        w = ge[:, j:j + 1]
        for b in range(2):
            r = slice(b * 16, (b + 1) * 16)
            v = ab[p, r, :] if j == 0 else rb[j, r, :]
            acc[b] = acc[b] + v * w
    si[p, c, :, :] = jnp.concatenate(acc, axis=0).astype(BF16)

    def gather(buf, k):
        own = remote(buf.at[p, c], buf.at[p, c], f_send.at[k, 0], f_recv.at[k, 0], peer)
        out = {
            j: remote(buf.at[p, c], buf.at[p, c], s_send.at[k, j], s_recv.at[k, j], (chip_of(j) * 2 + c, x))
            for j in range(1, CHIPS)
        }
        fwd = [own]
        for j in range(1, CHIPS):
            out[j].wait_recv()
            at = chip_from(j)
            fwd.append(remote(buf.at[at, c], buf.at[at, c], f_send.at[k, j], f_recv.at[k, j], peer))
        for cp in fwd:
            cp.wait_recv()

    gather(si, 1)

    xh = {}
    for d in (2, 1, 3, 0):
        q = lax.rem(x + d, 4)
        ld_win[d].wait()
        for k in range(2):
            e = 2 * q + k
            rows = jnp.concatenate(
                [si[e * 2 + h, g, b * 16:(b + 1) * 16, :] for h in range(2) for g in range(2) for b in range(2)],
                axis=1,
            )
            hp[d, k * 16:(k + 1) * 16, :] = jnp.dot(rows, win[e], preferred_element_type=F32)
        if d:
            xh[d] = remote(hp.at[d], hr.at[d], x_send.at[3, d], x_recv.at[3, d], xdev(d))
    hidden = hp[0]
    for d in (1, 3, 2):
        xh[d].wait_recv()
        hidden = hidden + hr[d]
    hidden = 0.5 * hidden * (1.0 + lax.erf(hidden * 0.7071067811865476))
    hb[x] = hidden.astype(BF16)
    xg = {d: remote(hb.at[x], hb.at[x], x_send.at[4, d], x_recv.at[4, d], xdev(d)) for d in SENDS}

    for d in ARRIVALS:
        q = lax.rem(x + 4 - d, 4)
        if d:
            xg[d].wait_recv()
        ld_wout[d].wait()
        for k in range(2):
            e = 2 * q + k
            o = jnp.dot(hb[q, k * 16:(k + 1) * 16, :], wout[e], preferred_element_type=F32)
            for h in range(2):
                for g in range(2):
                    for b in range(2):
                        at = h * 512 + g * 256 + b * 128
                        ob[g, e * 2 + h, b * 16:(b + 1) * 16, :] = o[:, at:at + 128]
    co = remote(ob.at[1 - c], po, c_send.at[1], c_recv.at[1], peer)
    co.wait_recv()
    ab2[...] = ob[c] + po[...]
    sv = {
        j: remote(ab2.at[chip_of(j)], ro.at[j], s_send.at[2, j], s_recv.at[2, j], (chip_of(j) * 2 + c, x))
        for j in range(1, CHIPS)
    }

    for d in (1, 3, 2):
        xn[d].wait_recv()
    cs = nsend[0, QT:QT + 8, :] + nrecv[1, QT:QT + 8, :] + nrecv[2, QT:QT + 8, :] + nrecv[3, QT:QT + 8, :]
    cnn = jnp.sqrt(jnp.sum(cs, axis=0, keepdims=True) + EPS)
    for g in range(4):
        r = slice(g * 64, (g + 1) * 64)
        rg = rnv[r, :]
        lwin = lw[r, :]
        ls = []
        top = lwin
        for b in range(7):
            at = slice(b * 128, (b + 1) * 128)
            raw = nsend[0, r, at] + nrecv[1, r, at] + nrecv[2, r, at] + nrecv[3, r, at]
            lg = scale * raw / (rg * cnn[:, at])
            ls.append(lg)
            top = jnp.maximum(top, lg)
        tmax = jnp.max(top, axis=1, keepdims=True)
        ew = jnp.exp(lwin - tmax)
        tsum = ew
        for lg in ls:
            tsum = tsum + jnp.exp(lg - tmax)
        ttot = jnp.sum(tsum, axis=1, keepdims=True)
        cb[x, r, :] = (ew / ttot).astype(BF16)
    xc = {d: remote(cb.at[x], cb.at[x], x_send.at[5, d], x_recv.at[5, d], xdev(d)) for d in SENDS}

    for j in range(1, CHIPS):
        sv[j].wait_recv()
    acc = ab2[p]
    for j in range(1, CHIPS):
        acc = acc + ro[j]
    so[p, c, :, :] = acc.astype(BF16)
    gather(so, 3)
    for d in SENDS:
        xc[d].wait_recv()
    for q in range(4):
        comb_o[q * QT:(q + 1) * QT, :] = cb[q]
    for e in range(E_RUN):
        for h in range(2):
            for g in range(2):
                for b in range(2):
                    at = h * 512 + g * 256 + b * 128
                    so_o[e * 16:(e + 1) * 16, at:at + 128] = so[e * 2 + h, g, b * 16:(b + 1) * 16, :]
    for cp in pending:
        cp.wait_send()


def per_device(tokens, slot_param, scale, w_in, w_out):
    vm = pltpu.VMEM
    dma = pltpu.SemaphoreType.DMA
    anyspec = pl.BlockSpec(memory_space=pl.ANY)
    vspec = pl.BlockSpec(memory_space=pltpu.VMEM)
    comb, slot_out = pl.pallas_call(
        kernel,
        name="moe_exchange",
        out_shape=(jax.ShapeDtypeStruct((1024, 128), BF16), jax.ShapeDtypeStruct((128, 1024), BF16)),
        in_specs=[anyspec, anyspec, pl.BlockSpec(memory_space=pltpu.SMEM), anyspec, anyspec],
        out_specs=(vspec, vspec),
        scratch_shapes=[
            vm((1024, 1024), BF16), vm((1024, 128), BF16), vm((1024, REST), BF16),
            vm((8, 1024, 512), BF16), vm((8, 512, 1024), BF16),
            vm((4, QT + 8, 128), F32), vm((4, QT + 8, 128), F32), vm((QT, 128), F32), vm((QT, 128), F32),
            vm((4, QT + 16, 128), BF16),
            vm((4, QT + 8, REST), F32), vm((4, QT + 8, REST), F32),
            vm((2, 16, 40, 128), F32), vm((16, 40, 128), F32), vm((16, 40, 128), F32), vm((16, 40, 128), F32),
            vm((128, 128), F32), vm((16, 2, 32, 128), BF16),
            vm((4, 32, 512), F32), vm((4, 32, 512), F32), vm((4, 32, 512), BF16),
            vm((2, 16, 32, 128), F32), vm((16, 32, 128), F32), vm((16, 32, 128), F32), vm((16, 32, 128), F32),
            vm((16, 2, 32, 128), BF16), vm((4, QT, 128), BF16),
            dma((14,)), dma((6, 4)), dma((6, 4)), dma((2,)), dma((2,)),
            dma((4, 16)), dma((4, 16)), dma((4, 16)), dma((4, 16)),
        ],
        compiler_params=pltpu.CompilerParams(
            collective_id=0, has_side_effects=True, vmem_limit_bytes=56 * 2**20
        ),
    )(tokens, slot_param, scale, w_in, w_out)
    return jnp.dot(comb, slot_out, preferred_element_type=F32).astype(BF16)


def solution(mesh):
    in_specs = (
        P("seq", "width"),
        P("width", None),
        P(),
        P(None, "width", "seq"),
        P(None, "seq", "width"),
    )
    return jax.shard_map(
        per_device, mesh=mesh, in_specs=in_specs, out_specs=P("seq", "width"), check_vma=False
    )
```

```python
import jax
import jax.numpy as jnp
from jax import lax
from jax.experimental import pallas as pl
from jax.experimental.pallas import tpu as pltpu
from jax.sharding import PartitionSpec as P

SLOT_PER = 16
E_RUN = 8
WINDOW = 128
EPS = 1e-06
F32 = jnp.float32
BF16 = jnp.bfloat16
MESH = pl.DeviceIdType.MESH
QT = 256
REST = 896
CHIPS = 16
SENDS = (2, 1, 3)
ARRIVALS = (0, 1, 3, 2)
GROUPS = (0, 1, 3, 2)


def column(row):
    return jnp.transpose(jnp.broadcast_to(row, (128, 128)))


def kernel(
    tok_h, sp_h, scale_ref, win_h, wout_h,
    comb_o, so_o,
    tok, spw, spn, win, wout,
    wsend, wrecv, lw, rnv, dsp, nsend, nrecv, relay_a, relay_b,
    wb, pr, ab, rb, gs, si,
    hp, hr, hb, ob, po, ab2, ro, so, cb,
    ld_sem, x_send, x_recv, c_send, c_recv, s_send, s_recv, f_send, f_recv,
):
    s = lax.axis_index("seq")
    x = lax.axis_index("width")
    c = lax.rem(s, 2)
    p = lax.div(s, 2)
    z = lax.div(p, 4)
    y = lax.rem(p, 4)
    peer = (s + 1 - 2 * c, x)

    def xdev(d):
        return (s, lax.rem(x + d, 4))

    def chip_of(j):
        return lax.rem(z + j // 4, 4) * 4 + lax.rem(y + j % 4, 4)

    def chip_from(j):
        return lax.rem(z + 4 - j // 4, 4) * 4 + lax.rem(y + 4 - j % 4, 4)

    pending = []

    def remote(src, dst, send, recv, to):
        cp = pltpu.make_async_remote_copy(
            src_ref=src, dst_ref=dst, send_sem=send, recv_sem=recv, device_id=to, device_id_type=MESH
        )
        cp.start()
        pending.append((None, cp))
        return cp

    def remote_if(cond, src, dst, send, recv, to):
        cp = pltpu.make_async_remote_copy(
            src_ref=src, dst_ref=dst, send_sem=send, recv_sem=recv, device_id=to, device_id_type=MESH
        )
        pl.when(cond)(cp.start)
        pending.append((cond, cp))

    def arrival(dst, send, recv):
        return pltpu.make_async_remote_copy(
            src_ref=dst, dst_ref=dst, send_sem=send, recv_sem=recv, device_id=peer, device_id_type=MESH
        )

    def load(src, dst, i):
        cp = pltpu.make_async_copy(src, dst, ld_sem.at[i])
        cp.start()
        return cp

    ld_spw = load(sp_h.at[:, pl.ds(0, WINDOW)], spw, 0)
    ld_tok = {}
    for i, d in enumerate((2, 1, 3, 0)):
        rows = pl.ds(lax.rem(x + d, 4) * QT, QT)
        ld_tok[d] = load(tok_h.at[rows], tok.at[rows], 1 + i)
    ld_spn = load(sp_h.at[:, pl.ds(WINDOW, REST)], spn, 5)
    barrier = pltpu.get_barrier_semaphore()
    for d in (1, 2, 3):
        pl.semaphore_signal(barrier, inc=1, device_id=xdev(d), device_id_type=MESH)
    pl.semaphore_signal(barrier, inc=1, device_id=peer, device_id_type=MESH)
    for j in range(1, CHIPS):
        pl.semaphore_signal(barrier, inc=1, device_id=(chip_of(j) * 2 + c, x), device_id_type=MESH)

    ld_spw.wait()
    spf = spw[...].astype(F32)
    csq = jnp.sum(spf * spf, axis=0, keepdims=True)
    xw = {}
    for d in (2, 1, 3, 0):
        ld_tok[d].wait()
        t = tok[pl.ds(lax.rem(x + d, 4) * QT, QT), :]
        wsend[d, 0:QT, :] = jnp.dot(t, spw[...], preferred_element_type=F32)
        part = jnp.zeros((QT, 128), F32)
        for b in range(8):
            tf = t[:, b * 128:(b + 1) * 128].astype(F32)
            part = part + tf * tf
        rows = [jnp.sum(jnp.transpose(part[h * 128:(h + 1) * 128]), axis=0, keepdims=True) for h in range(2)]
        wsend[d, QT:QT + 8, :] = jnp.concatenate(rows + [csq, jnp.zeros((5, 128), F32)], axis=0)
        if d == 2:
            pl.semaphore_wait(barrier, 19)
        if d:
            xw[d] = remote(wsend.at[d], wrecv.at[d], x_send.at[0, d], x_recv.at[0, d], xdev(d))
    ld_win = {}
    for i, dz in enumerate(GROUPS):
        e = 2 * lax.rem(z + 4 - dz, 4)
        ld_win[dz] = load(win_h.at[pl.ds(e, 2)], win.at[pl.ds(e, 2)], 6 + i)
    ld_wout = {}
    for i, d in enumerate(ARRIVALS):
        e = 2 * lax.rem(x + 4 - d, 4)
        ld_wout[d] = load(wout_h.at[pl.ds(e, 2)], wout.at[pl.ds(e, 2)], 10 + i)

    ld_spn.wait()
    csn = jnp.zeros((8, REST), F32)
    for b in range(32):
        sf = spn[b * 32:(b + 1) * 32, :].astype(F32)
        sq = sf * sf
        csn = csn + sq[0:8] + sq[8:16] + sq[16:24] + sq[24:32]
    for d in (2, 1, 3, 0):
        t = tok[pl.ds(lax.rem(x + d, 4) * QT, QT), :]
        nsend[d, 0:QT, :] = jnp.dot(t, spn[...], preferred_element_type=F32)
        nsend[d, QT:QT + 8, :] = csn

    tot = wsend[0]
    for d in (1, 3, 2):
        xw[d].wait_recv()
        tot = tot + wrecv[d]
    rn = jnp.sqrt(jnp.concatenate([column(tot[QT:QT + 1]), column(tot[QT + 1:QT + 2])], axis=0) + EPS)
    cn = jnp.sqrt(tot[QT + 2:QT + 3] + EPS)
    scale = scale_ref[0]
    logits = scale * tot[0:QT] / (rn * cn)
    lw[...] = logits
    rnv[...] = rn
    m = jnp.max(logits, axis=0, keepdims=True).astype(BF16)
    dsp[x, 0:QT, :] = jnp.exp(logits - m.astype(F32)).astype(BF16)
    dsp[x, QT:QT + 16, :] = jnp.broadcast_to(m, (16, 128))
    xd = {d: remote(dsp.at[x], dsp.at[x], x_send.at[1, d], x_recv.at[1, d], xdev(d)) for d in SENDS}

    for d in SENDS:
        xd[d].wait_recv()
    low, high = pl.ds(0, 128), pl.ds(128, QT + 8 - 128)
    via_a = remote(nsend.at[2, low], relay_a, x_send.at[2, 0], x_recv.at[2, 0], xdev(1))
    via_b = remote(nsend.at[2, high], relay_b, x_send.at[2, 1], x_recv.at[2, 1], xdev(3))
    xn = [
        remote(nsend.at[1, high], nrecv.at[0, high], x_send.at[2, 2], x_recv.at[2, 2], xdev(1)),
        remote(nsend.at[3, low], nrecv.at[1, low], x_send.at[2, 3], x_recv.at[2, 3], xdev(3)),
    ]
    ms = [dsp[q, QT:QT + 1, :].astype(F32) for q in range(4)]
    mseq = jnp.maximum(jnp.maximum(ms[0], ms[1]), jnp.maximum(ms[2], ms[3]))
    total = jnp.zeros((1, 128), F32)
    cols = []
    for q in range(4):
        f = jnp.exp(ms[q] - mseq)
        total = total + f * jnp.sum(dsp[q, 0:QT, :].astype(F32), axis=0, keepdims=True)
        cols.append(column(f))
    stats = jnp.concatenate([mseq, total, jnp.zeros((6, 128), F32)], axis=0)
    cw = None
    for k in (1 - c, c):
        for h in range(2):
            at = pl.multiple_of(h * 512 + k * 256, 256)
            acc = jnp.zeros((128, 256), F32)
            for q in range(4):
                prod = lax.dot_general(
                    dsp[q, 0:QT, :], tok[q * QT:(q + 1) * QT, pl.ds(at, 256)],
                    (((0,), (0,)), ((), ())), preferred_element_type=F32,
                )
                acc = acc + prod * jnp.concatenate([cols[q], cols[q]], axis=1)
            for e in range(E_RUN):
                for b in range(2):
                    wb[k, e * 2 + h, b * 16:(b + 1) * 16, :] = acc[e * 16:(e + 1) * 16, b * 128:(b + 1) * 128]
                wb[k, e * 2 + h, 32:40, :] = stats
        if cw is None:
            cw = remote(wb.at[1 - c], pr, c_send.at[0], c_recv.at[0], peer)

    cw.wait_recv()
    m_a, m_b = wb[c, 0, 32:33, :], pr[0, 32:33, :]
    m2 = jnp.maximum(m_a, m_b)
    f_a, f_b = jnp.exp(m_a - m2), jnp.exp(m_b - m2)
    t2 = f_a * wb[c, 0, 33:34, :] + f_b * pr[0, 33:34, :]
    stats = jnp.concatenate([m2, t2, jnp.zeros((6, 128), F32)], axis=0)
    c_a, c_b = column(f_a), column(f_b)
    for i in range(CHIPS):
        e = i // 2
        k_a, k_b = c_a[e * 16:(e + 1) * 16], c_b[e * 16:(e + 1) * 16]
        for b in range(2):
            r = slice(b * 16, (b + 1) * 16)
            ab[i, r, :] = wb[c, i, r, :] * k_a + pr[i, r, :] * k_b
        ab[i, 32:40, :] = stats
    sw = {
        j: remote(ab.at[chip_of(j)], rb.at[j], s_send.at[0, j], s_recv.at[0, j], (chip_of(j) * 2 + c, x))
        for j in range(1, CHIPS)
    }
    for j in range(1, CHIPS):
        sw[j].wait_recv()
    mr = [ab[p, 32:33, :]] + [rb[j, 32:33, :] for j in range(1, CHIPS)]
    tr = [ab[p, 33:34, :]] + [rb[j, 33:34, :] for j in range(1, CHIPS)]
    top = mr[0]
    for v in mr[1:]:
        top = jnp.maximum(top, v)
    fr = [jnp.exp(v - top) for v in mr]
    total = fr[0] * tr[0]
    for f, t in zip(fr[1:], tr[1:]):
        total = total + f * t
    gs[...] = jnp.transpose(jnp.concatenate([f / total for f in fr] + [jnp.zeros((112, 128), F32)], axis=0))
    ge = gs[pl.ds(lax.div(p, 2) * 16, 16), :]
    acc = [jnp.zeros((16, 128), F32)] * 2
    for j in range(CHIPS):
        w = ge[:, j:j + 1]
        for b in range(2):
            r = slice(b * 16, (b + 1) * 16)
            v = ab[p, r, :] if j == 0 else rb[j, r, :]
            acc[b] = acc[b] + v * w
    si[p, c, :, :] = jnp.concatenate(acc, axis=0).astype(BF16)


    def gather(buf, k):
        fwd = {0: remote(buf.at[p, c], buf.at[p, c], f_send.at[k, 0], f_recv.at[k, 0], peer)}
        out = {
            j: remote(buf.at[p, c], buf.at[p, c], s_send.at[k, j], s_recv.at[k, j], (chip_of(j) * 2 + c, x))
            for j in range(1, CHIPS)
        }

        def arrive(dz):
            for j in range(dz * 4, dz * 4 + 4):
                if j:
                    out[j].wait_recv()
                    at = chip_from(j)
                    fwd[j] = remote(buf.at[at, c], buf.at[at, c], f_send.at[k, j], f_recv.at[k, j], peer)

        def whole(dz):
            for j in range(dz * 4, dz * 4 + 4):
                fwd[j].wait_recv()

        return arrive, whole

    arrive, whole = gather(si, 1)

    arrive(GROUPS[0])
    for i, dz in enumerate(GROUPS):
        if i < 3:
            arrive(GROUPS[i + 1])
        whole(dz)
        q = lax.rem(z + 4 - dz, 4)
        d = lax.rem(q + 4 - x, 4)
        ld_win[dz].wait()
        for k in range(2):
            e = 2 * q + k
            rows = jnp.concatenate(
                [si[e * 2 + h, g, b * 16:(b + 1) * 16, :] for h in range(2) for g in range(2) for b in range(2)],
                axis=1,
            )
            hp[dz, k * 16:(k + 1) * 16, :] = jnp.dot(rows, win[e], preferred_element_type=F32)
        remote_if(d != 0, hp.at[dz], hr.at[d], x_send.at[3, dz], x_recv.at[3, d], (s, q))

        @pl.when(d == 0)
        def _(dz=dz):
            hr[0] = hp[dz]

    xh = {d: arrival(hr.at[d], x_send.at[3, 0], x_recv.at[3, d]) for d in (1, 2, 3)}
    hidden = hr[0]
    for d in (1, 3, 2):
        xh[d].wait_recv()
        hidden = hidden + hr[d]
    hidden = 0.5 * hidden * (1.0 + lax.erf(hidden * 0.7071067811865476))
    hb[x] = hidden.astype(BF16)
    xg = {d: remote(hb.at[x], hb.at[x], x_send.at[4, d], x_recv.at[4, d], xdev(d)) for d in SENDS}

    def chips_sum(q, copy):
        copy.wait_recv()
        block = pl.ds(4 * q, 4)
        ab2[block] = ob[c, block] + po[block]
        dz = lax.rem(q + 4 - z, 4)
        for dy in range(4):
            to = q * 4 + lax.rem(y + dy, 4)
            j = dz * 4 + dy
            args = (ab2.at[to], ro.at[j], s_send.at[2, j], s_recv.at[2, j], (to * 2 + c, x))
            if dy:
                remote(*args)
            else:
                remote_if(dz != 0, *args)

    last = None
    for i, d in enumerate(ARRIVALS):
        q = lax.rem(x + 4 - d, 4)
        if d:
            xg[d].wait_recv()
        ld_wout[d].wait()
        for k in range(2):
            e = 2 * q + k
            o = jnp.dot(hb[q, k * 16:(k + 1) * 16, :], wout[e], preferred_element_type=F32)
            for h in range(2):
                for g in range(2):
                    for b in range(2):
                        at = h * 512 + g * 256 + b * 128
                        ob[g, e * 2 + h, b * 16:(b + 1) * 16, :] = o[:, at:at + 128]
        block = pl.ds(4 * q, 4)
        copy = remote(ob.at[1 - c, block], po.at[block], c_send.at[1 + i], c_recv.at[1 + i], peer)
        if last is not None:
            chips_sum(*last)
        last = (q, copy)
        if d == 0:
            via_a.wait_recv()
            nsend[1, low, :] = nsend[1, low, :] + relay_a[...]
            xn.append(remote(nsend.at[1, low], nrecv.at[0, low], x_send.at[6, 0], x_recv.at[6, 0], xdev(1)))
            via_b.wait_recv()
            nsend[3, high, :] = nsend[3, high, :] + relay_b[...]
            xn.append(remote(nsend.at[3, high], nrecv.at[1, high], x_send.at[6, 1], x_recv.at[6, 1], xdev(3)))
    chips_sum(*last)
    sv = {j: arrival(ro.at[j], s_send.at[2, 0], s_recv.at[2, j]) for j in range(1, CHIPS)}
    for cp in xn:
        cp.wait_recv()
    cs = nsend[0, QT:QT + 8, :] + nrecv[0, QT:QT + 8, :] + nrecv[1, QT:QT + 8, :]
    cnn = jnp.sqrt(jnp.sum(cs, axis=0, keepdims=True) + EPS)
    for g in range(4):
        r = slice(g * 64, (g + 1) * 64)
        rg = rnv[r, :]
        lwin = lw[r, :]
        ls = []
        top = lwin
        for b in range(7):
            at = slice(b * 128, (b + 1) * 128)
            raw = nsend[0, r, at] + nrecv[0, r, at] + nrecv[1, r, at]
            lg = scale * raw / (rg * cnn[:, at])
            ls.append(lg)
            top = jnp.maximum(top, lg)
        tmax = jnp.max(top, axis=1, keepdims=True)
        ew = jnp.exp(lwin - tmax)
        tsum = ew
        for lg in ls:
            tsum = tsum + jnp.exp(lg - tmax)
        ttot = jnp.sum(tsum, axis=1, keepdims=True)
        cb[x, r, :] = (ew / ttot).astype(BF16)
    xc = {d: remote(cb.at[x], cb.at[x], x_send.at[5, d], x_recv.at[5, d], xdev(d)) for d in SENDS}

    for j in range(1, CHIPS):
        sv[j].wait_recv()
    acc = ab2[p]
    for j in range(1, CHIPS):
        acc = acc + ro[j]
    so[p, c, :, :] = acc.astype(BF16)
    arrive, whole = gather(so, 3)
    for dz in GROUPS:
        arrive(dz)
    for dz in GROUPS:
        whole(dz)
    for d in SENDS:
        xc[d].wait_recv()
    for q in range(4):
        comb_o[q * QT:(q + 1) * QT, :] = cb[q]
    for e in range(E_RUN):
        for h in range(2):
            for g in range(2):
                for b in range(2):
                    at = h * 512 + g * 256 + b * 128
                    so_o[e * 16:(e + 1) * 16, at:at + 128] = so[e * 2 + h, g, b * 16:(b + 1) * 16, :]
    for cond, cp in pending:
        if cond is None:
            cp.wait_send()
        else:
            pl.when(cond)(cp.wait_send)


def per_device(tokens, slot_param, scale, w_in, w_out):
    vm = pltpu.VMEM
    dma = pltpu.SemaphoreType.DMA
    anyspec = pl.BlockSpec(memory_space=pl.ANY)
    vspec = pl.BlockSpec(memory_space=pltpu.VMEM)
    comb, slot_out = pl.pallas_call(
        kernel,
        name="moe_exchange",
        out_shape=(jax.ShapeDtypeStruct((1024, 128), BF16), jax.ShapeDtypeStruct((128, 1024), BF16)),
        in_specs=[anyspec, anyspec, pl.BlockSpec(memory_space=pltpu.SMEM), anyspec, anyspec],
        out_specs=(vspec, vspec),
        scratch_shapes=[
            vm((1024, 1024), BF16), vm((1024, 128), BF16), vm((1024, REST), BF16),
            vm((8, 1024, 512), BF16), vm((8, 512, 1024), BF16),
            vm((4, QT + 8, 128), F32), vm((4, QT + 8, 128), F32), vm((QT, 128), F32), vm((QT, 128), F32),
            vm((4, QT + 16, 128), BF16),
            vm((4, QT + 8, REST), F32), vm((2, QT + 8, REST), F32), vm((128, REST), F32), vm((QT - 120, REST), F32),
            vm((2, 16, 40, 128), F32), vm((16, 40, 128), F32), vm((16, 40, 128), F32), vm((16, 40, 128), F32),
            vm((128, 128), F32), vm((16, 2, 32, 128), BF16),
            vm((4, 32, 512), F32), vm((4, 32, 512), F32), vm((4, 32, 512), BF16),
            vm((2, 16, 32, 128), F32), vm((16, 32, 128), F32), vm((16, 32, 128), F32), vm((16, 32, 128), F32),
            vm((16, 2, 32, 128), BF16), vm((4, QT, 128), BF16),
            dma((14,)), dma((7, 4)), dma((7, 4)), dma((5,)), dma((5,)),
            dma((4, 16)), dma((4, 16)), dma((4, 16)), dma((4, 16)),
        ],
        compiler_params=pltpu.CompilerParams(
            collective_id=0, has_side_effects=True, vmem_limit_bytes=56 * 2**20
        ),
    )(tokens, slot_param, scale, w_in, w_out)
    return jnp.dot(comb, slot_out, preferred_element_type=F32).astype(BF16)


def solution(mesh):
    in_specs = (
        P("seq", "width"),
        P("width", None),
        P(),
        P(None, "width", "seq"),
        P(None, "seq", "width"),
    )
    return jax.shard_map(
        per_device, mesh=mesh, in_specs=in_specs, out_specs=P("seq", "width"), check_vma=False
    )
```

```python
import jax
import jax.numpy as jnp
from jax import lax
from jax.experimental import pallas as pl
from jax.experimental.pallas import tpu as pltpu
from jax.sharding import PartitionSpec as P

SLOT_PER = 16
E_RUN = 8
WINDOW = 128
EPS = 1e-06
F32 = jnp.float32
BF16 = jnp.bfloat16
MESH = pl.DeviceIdType.MESH
QT = 256
REST = 896
CHIPS = 16
SENDS = (2, 1, 3)
ARRIVALS = (0, 1, 3, 2)
GROUPS = (0, 1, 3, 2)


def column(row):
    return jnp.transpose(jnp.broadcast_to(row, (128, 128)))


def kernel(
    tok_h, sp_h, scale_ref, win_h, wout_h,
    comb_o, so_o,
    tok, spw, spn, win, wout,
    wsend, wrecv, lw, rnv, dsp, nsend, nrecv, relay_a, relay_b,
    wb, pr, ab, rb, gs, si,
    hp, hr, h_own, hb, ob, po, ab2, ro, so, cb,
    ld_sem, x_send, x_recv, c_send, c_recv, s_send, s_recv, f_send, f_recv,
):
    s = lax.axis_index("seq")
    x = lax.axis_index("width")
    c = lax.rem(s, 2)
    p = lax.div(s, 2)
    z = lax.div(p, 4)
    y = lax.rem(p, 4)
    peer = (s + 1 - 2 * c, x)

    def xdev(d):
        return (s, lax.rem(x + d, 4))

    def chip_of(j):
        return lax.rem(z + j // 4, 4) * 4 + lax.rem(y + j % 4, 4)

    def chip_from(j):
        return lax.rem(z + 4 - j // 4, 4) * 4 + lax.rem(y + 4 - j % 4, 4)

    pending = []

    def remote(src, dst, send, recv, to):
        cp = pltpu.make_async_remote_copy(
            src_ref=src, dst_ref=dst, send_sem=send, recv_sem=recv, device_id=to, device_id_type=MESH
        )
        cp.start()
        pending.append((None, cp))
        return cp

    def remote_if(cond, src, dst, send, recv, to):
        cp = pltpu.make_async_remote_copy(
            src_ref=src, dst_ref=dst, send_sem=send, recv_sem=recv, device_id=to, device_id_type=MESH
        )
        pl.when(cond)(cp.start)
        pending.append((cond, cp))
        return cp

    def sent(copies):
        for cp in copies:
            for k, (cond, other) in enumerate(pending):
                if other is cp:
                    del pending[k]
                    break
            if cond is None:
                cp.wait_send()
            else:
                pl.when(cond)(cp.wait_send)

    xn = []

    def piece(d, start, count, k):
        rows, slot = pl.ds(start, count), d // 2
        xn.append(remote(nsend.at[d, rows], nrecv.at[slot, rows], x_send.at[k, slot], x_recv.at[k, slot], xdev(d)))

    def arrival(dst, send, recv):
        return pltpu.make_async_remote_copy(
            src_ref=dst, dst_ref=dst, send_sem=send, recv_sem=recv, device_id=peer, device_id_type=MESH
        )

    def load(src, dst, i):
        cp = pltpu.make_async_copy(src, dst, ld_sem.at[i])
        cp.start()
        return cp

    ld_spw = load(sp_h.at[:, pl.ds(0, WINDOW)], spw, 0)
    ld_tok = {}
    for i, d in enumerate((2, 1, 3, 0)):
        rows = pl.ds(lax.rem(x + d, 4) * QT, QT)
        ld_tok[d] = load(tok_h.at[rows], tok.at[rows], 1 + i)
    ld_spn = load(sp_h.at[:, pl.ds(WINDOW, REST)], spn, 5)
    barrier = pltpu.get_barrier_semaphore()
    for d in (1, 2, 3):
        pl.semaphore_signal(barrier, inc=1, device_id=xdev(d), device_id_type=MESH)
    pl.semaphore_signal(barrier, inc=1, device_id=peer, device_id_type=MESH)
    for j in range(1, CHIPS):
        pl.semaphore_signal(barrier, inc=1, device_id=(chip_of(j) * 2 + c, x), device_id_type=MESH)

    ld_spw.wait()
    spf = spw[...].astype(F32)
    csq = jnp.sum(spf * spf, axis=0, keepdims=True)
    xw = {}
    for d in (2, 1, 3, 0):
        ld_tok[d].wait()
        t = tok[pl.ds(lax.rem(x + d, 4) * QT, QT), :]
        wsend[d, 0:QT, :] = jnp.dot(t, spw[...], preferred_element_type=F32)
        part = jnp.zeros((QT, 128), F32)
        for b in range(8):
            tf = t[:, b * 128:(b + 1) * 128].astype(F32)
            part = part + tf * tf
        rows = [jnp.sum(jnp.transpose(part[h * 128:(h + 1) * 128]), axis=0, keepdims=True) for h in range(2)]
        wsend[d, QT:QT + 8, :] = jnp.concatenate(rows + [csq, jnp.zeros((5, 128), F32)], axis=0)
        if d == 2:
            pl.semaphore_wait(barrier, 19)
        if d:
            xw[d] = remote(wsend.at[d], wrecv.at[d], x_send.at[0, d], x_recv.at[0, d], xdev(d))
    ld_win = {}
    for i, dz in enumerate(GROUPS):
        e = 2 * lax.rem(z + 4 - dz, 4)
        ld_win[dz] = load(win_h.at[pl.ds(e, 2)], win.at[pl.ds(e, 2)], 6 + i)
    ld_wout = {}
    for i, d in enumerate(ARRIVALS):
        e = 2 * lax.rem(x + 4 - d, 4)
        ld_wout[d] = load(wout_h.at[pl.ds(e, 2)], wout.at[pl.ds(e, 2)], 10 + i)

    ld_spn.wait()
    csn = jnp.zeros((8, REST), F32)
    for b in range(32):
        sf = spn[b * 32:(b + 1) * 32, :].astype(F32)
        sq = sf * sf
        csn = csn + sq[0:8] + sq[8:16] + sq[16:24] + sq[24:32]
    for d in (2, 1, 3, 0):
        t = tok[pl.ds(lax.rem(x + d, 4) * QT, QT), :]
        nsend[d, 0:QT, :] = jnp.dot(t, spn[...], preferred_element_type=F32)
        nsend[d, QT:QT + 8, :] = csn

    sent(list(xw.values()))
    piece(1, 128, 32, 6)
    piece(3, 0, 32, 6)
    tot = wsend[0]
    for d in (1, 3, 2):
        xw[d].wait_recv()
        tot = tot + wrecv[d]
    rn = jnp.sqrt(jnp.concatenate([column(tot[QT:QT + 1]), column(tot[QT + 1:QT + 2])], axis=0) + EPS)
    cn = jnp.sqrt(tot[QT + 2:QT + 3] + EPS)
    scale = scale_ref[0]
    logits = scale * tot[0:QT] / (rn * cn)
    lw[...] = logits
    rnv[...] = rn
    m = jnp.max(logits, axis=0, keepdims=True).astype(BF16)
    dsp[x, 0:QT, :] = jnp.exp(logits - m.astype(F32)).astype(BF16)
    dsp[x, QT:QT + 16, :] = jnp.broadcast_to(m, (16, 128))
    xd = {d: remote(dsp.at[x], dsp.at[x], x_send.at[1, d], x_recv.at[1, d], xdev(d)) for d in SENDS}

    sent(list(xd.values()))
    piece(1, 160, 32, 7)
    piece(3, 32, 32, 7)
    for d in SENDS:
        xd[d].wait_recv()
    via_a = remote(nsend.at[2, pl.ds(0, 128)], relay_a, x_send.at[2, 0], x_recv.at[2, 0], xdev(1))
    via_b = remote(nsend.at[2, pl.ds(128, 136)], relay_b, x_send.at[2, 1], x_recv.at[2, 1], xdev(3))
    ms = [dsp[q, QT:QT + 1, :].astype(F32) for q in range(4)]
    mseq = jnp.maximum(jnp.maximum(ms[0], ms[1]), jnp.maximum(ms[2], ms[3]))
    total = jnp.zeros((1, 128), F32)
    cols = []
    for q in range(4):
        f = jnp.exp(ms[q] - mseq)
        total = total + f * jnp.sum(dsp[q, 0:QT, :].astype(F32), axis=0, keepdims=True)
        cols.append(column(f))
    stats = jnp.concatenate([mseq, total, jnp.zeros((6, 128), F32)], axis=0)
    cw = None
    for k in (1 - c, c):
        for h in range(2):
            at = pl.multiple_of(h * 512 + k * 256, 256)
            acc = jnp.zeros((128, 256), F32)
            for q in range(4):
                prod = lax.dot_general(
                    dsp[q, 0:QT, :], tok[q * QT:(q + 1) * QT, pl.ds(at, 256)],
                    (((0,), (0,)), ((), ())), preferred_element_type=F32,
                )
                acc = acc + prod * jnp.concatenate([cols[q], cols[q]], axis=1)
            for e in range(E_RUN):
                for b in range(2):
                    wb[k, e * 2 + h, b * 16:(b + 1) * 16, :] = acc[e * 16:(e + 1) * 16, b * 128:(b + 1) * 128]
                wb[k, e * 2 + h, 32:40, :] = stats
        if cw is None:
            cw = remote(wb.at[1 - c], pr, c_send.at[0], c_recv.at[0], peer)

    cw.wait_recv()
    m_a, m_b = wb[c, 0, 32:33, :], pr[0, 32:33, :]
    m2 = jnp.maximum(m_a, m_b)
    f_a, f_b = jnp.exp(m_a - m2), jnp.exp(m_b - m2)
    t2 = f_a * wb[c, 0, 33:34, :] + f_b * pr[0, 33:34, :]
    t_hi = t2.astype(BF16).astype(F32)
    stats = jnp.concatenate([m2, t_hi, t2 - t_hi, jnp.zeros((13, 128), F32)], axis=0).astype(BF16)
    c_a, c_b = column(f_a), column(f_b)
    for i in range(CHIPS):
        e = i // 2
        k_a, k_b = c_a[e * 16:(e + 1) * 16], c_b[e * 16:(e + 1) * 16]
        for b in range(2):
            r = slice(b * 16, (b + 1) * 16)
            ab[i, r, :] = (wb[c, i, r, :] * k_a + pr[i, r, :] * k_b).astype(BF16)
        ab[i, 32:48, :] = stats
    sw = {
        j: remote(ab.at[chip_of(j)], rb.at[j], s_send.at[0, j], s_recv.at[0, j], (chip_of(j) * 2 + c, x))
        for j in range(1, CHIPS)
    }
    for j in range(1, CHIPS):
        sw[j].wait_recv()
    piece(1, 192, 72, 8)
    piece(3, 64, 64, 8)
    st = [ab[p, 32:48, :].astype(F32)] + [rb[j, 32:48, :].astype(F32) for j in range(1, CHIPS)]
    mr = [v[0:1] for v in st]
    tr = [v[1:2] + v[2:3] for v in st]
    top = mr[0]
    for v in mr[1:]:
        top = jnp.maximum(top, v)
    fr = [jnp.exp(v - top) for v in mr]
    total = fr[0] * tr[0]
    for f, t in zip(fr[1:], tr[1:]):
        total = total + f * t
    gs[...] = jnp.transpose(jnp.concatenate([f / total for f in fr] + [jnp.zeros((112, 128), F32)], axis=0))
    ge = gs[pl.ds(lax.div(p, 2) * 16, 16), :]
    acc = [jnp.zeros((16, 128), F32)] * 2
    for j in range(CHIPS):
        w = ge[:, j:j + 1]
        for b in range(2):
            r = slice(b * 16, (b + 1) * 16)
            v = ab[p, r, :] if j == 0 else rb[j, r, :]
            acc[b] = acc[b] + v.astype(F32) * w
    si[p, c, :, :] = jnp.concatenate(acc, axis=0).astype(BF16)


    def gather(buf, k):
        fwd = {0: remote(buf.at[p, c], buf.at[p, c], f_send.at[k, 0], f_recv.at[k, 0], peer)}
        out = {
            j: remote(buf.at[p, c], buf.at[p, c], s_send.at[k, j], s_recv.at[k, j], (chip_of(j) * 2 + c, x))
            for j in range(1, CHIPS)
        }

        def arrive(dz):
            for j in range(dz * 4, dz * 4 + 4):
                if j:
                    out[j].wait_recv()
                    at = chip_from(j)
                    fwd[j] = remote(buf.at[at, c], buf.at[at, c], f_send.at[k, j], f_recv.at[k, j], peer)

        def whole(dz):
            for j in range(dz * 4, dz * 4 + 4):
                fwd[j].wait_recv()

        return arrive, whole

    arrive, whole = gather(si, 1)

    xp = []
    arrive(GROUPS[0])
    for i, dz in enumerate(GROUPS):
        if i < 3:
            arrive(GROUPS[i + 1])
        whole(dz)
        q = lax.rem(z + 4 - dz, 4)
        d = lax.rem(q + 4 - x, 4)
        ld_win[dz].wait()
        own = []
        for k in range(2):
            e = 2 * q + k
            rows = jnp.concatenate(
                [si[e * 2 + h, g, b * 16:(b + 1) * 16, :] for h in range(2) for g in range(2) for b in range(2)],
                axis=1,
            )
            own.append(jnp.dot(rows, win[e], preferred_element_type=F32))
        own = jnp.concatenate(own, axis=0)
        hp[dz] = own.astype(BF16)
        xp.append(remote_if(d != 0, hp.at[dz], hr.at[d], x_send.at[3, dz], x_recv.at[3, d], (s, q)))

        @pl.when(d == 0)
        def _(own=own):
            h_own[...] = own

    xh = {d: arrival(hr.at[d], x_send.at[3, 0], x_recv.at[3, d]) for d in (1, 2, 3)}
    via_a.wait_recv()
    nsend[1, 0:128, :] = nsend[1, 0:128, :] + relay_a[...]
    via_b.wait_recv()
    nsend[3, 128:264, :] = nsend[3, 128:264, :] + relay_b[...]
    sent(xp)
    piece(1, 0, 32, 9)
    piece(3, 128, 32, 9)
    hidden = h_own[...]
    for d in (1, 3, 2):
        xh[d].wait_recv()
        hidden = hidden + hr[d].astype(F32)
    hidden = 0.5 * hidden * (1.0 + lax.erf(hidden * 0.7071067811865476))
    hb[x] = hidden.astype(BF16)
    xg = {d: remote(hb.at[x], hb.at[x], x_send.at[4, d], x_recv.at[4, d], xdev(d)) for d in SENDS}

    sent(list(xg.values()))
    piece(1, 32, 96, 10)
    piece(3, 160, 104, 10)
    def chips_sum(q, copy):
        copy.wait_recv()
        block = pl.ds(4 * q, 4)
        ab2[block] = (ob[c, block] + po[block]).astype(BF16)
        dz = lax.rem(q + 4 - z, 4)
        for dy in range(4):
            to = q * 4 + lax.rem(y + dy, 4)
            j = dz * 4 + dy
            args = (ab2.at[to], ro.at[j], s_send.at[2, j], s_recv.at[2, j], (to * 2 + c, x))
            if dy:
                remote(*args)
            else:
                remote_if(dz != 0, *args)

    last = None
    for i, d in enumerate(ARRIVALS):
        q = lax.rem(x + 4 - d, 4)
        if d:
            xg[d].wait_recv()
        ld_wout[d].wait()
        for k in range(2):
            e = 2 * q + k
            o = jnp.dot(hb[q, k * 16:(k + 1) * 16, :], wout[e], preferred_element_type=F32)
            for h in range(2):
                for g in range(2):
                    for b in range(2):
                        at = h * 512 + g * 256 + b * 128
                        ob[g, e * 2 + h, b * 16:(b + 1) * 16, :] = o[:, at:at + 128]
        block = pl.ds(4 * q, 4)
        copy = remote(ob.at[1 - c, block], po.at[block], c_send.at[1 + i], c_recv.at[1 + i], peer)
        if last is not None:
            chips_sum(*last)
        last = (q, copy)
    chips_sum(*last)
    sv = {j: arrival(ro.at[j], s_send.at[2, 0], s_recv.at[2, j]) for j in range(1, CHIPS)}
    for j in range(1, CHIPS):
        sv[j].wait_recv()
    acc = ab2[p].astype(F32)
    for j in range(1, CHIPS):
        acc = acc + ro[j].astype(F32)
    so[p, c, :, :] = acc.astype(BF16)
    arrive, whole = gather(so, 3)

    for cp in xn:
        cp.wait_recv()
    cs = nsend[0, QT:QT + 8, :] + nrecv[0, QT:QT + 8, :] + nrecv[1, QT:QT + 8, :]
    cnn = jnp.sqrt(jnp.sum(cs, axis=0, keepdims=True) + EPS)
    for g in range(4):
        r = slice(g * 64, (g + 1) * 64)
        rg = rnv[r, :]
        lwin = lw[r, :]
        ls = []
        top = lwin
        for b in range(7):
            at = slice(b * 128, (b + 1) * 128)
            raw = nsend[0, r, at] + nrecv[0, r, at] + nrecv[1, r, at]
            lg = scale * raw / (rg * cnn[:, at])
            ls.append(lg)
            top = jnp.maximum(top, lg)
        tmax = jnp.max(top, axis=1, keepdims=True)
        ew = jnp.exp(lwin - tmax)
        tsum = ew
        for lg in ls:
            tsum = tsum + jnp.exp(lg - tmax)
        ttot = jnp.sum(tsum, axis=1, keepdims=True)
        cb[x, r, :] = (ew / ttot).astype(BF16)
    xc = {d: remote(cb.at[x], cb.at[x], x_send.at[5, d], x_recv.at[5, d], xdev(d)) for d in SENDS}

    for dz in GROUPS:
        arrive(dz)
    for d in SENDS:
        xc[d].wait_recv()
    store_comb = load(cb, comb_o, 14)
    for dz in GROUPS:
        whole(dz)
    load(so, so_o, 15).wait()
    store_comb.wait()
    for cond, cp in pending:
        if cond is None:
            cp.wait_send()
        else:
            pl.when(cond)(cp.wait_send)


def mix(comb_h, so_h, out_h, comb, so, slot_out, out, sem):
    def copy(src, dst, i):
        cp = pltpu.make_async_copy(src, dst, sem.at[i])
        cp.start()
        return cp

    ld_so = copy(so_h, so, 8)
    ld_comb = [copy(comb_h.at[g], comb.at[g], 4 + g) for g in range(4)]
    ld_so.wait()
    for e in range(E_RUN):
        for h in range(2):
            for g in range(2):
                for b in range(2):
                    at = h * 512 + g * 256 + b * 128
                    slot_out[e * 16:(e + 1) * 16, at:at + 128] = so[e * 2 + h, g, b * 16:(b + 1) * 16, :]
    stores = []
    for g in range(4):
        ld_comb[g].wait()
        r = pl.ds(g * QT, QT)
        out[r, :] = jnp.dot(comb[g], slot_out[...], preferred_element_type=F32).astype(BF16)
        stores.append(copy(out.at[r], out_h.at[r], g))
    for cp in stores:
        cp.wait()


def per_device(tokens, slot_param, scale, w_in, w_out):
    vm = pltpu.VMEM
    dma = pltpu.SemaphoreType.DMA
    anyspec = pl.BlockSpec(memory_space=pl.ANY)
    comb, slot_out = pl.pallas_call(
        kernel,
        name="moe_exchange",
        out_shape=(jax.ShapeDtypeStruct((4, QT, 128), BF16), jax.ShapeDtypeStruct((16, 2, 32, 128), BF16)),
        in_specs=[anyspec, anyspec, pl.BlockSpec(memory_space=pltpu.SMEM), anyspec, anyspec],
        out_specs=(anyspec, anyspec),
        scratch_shapes=[
            vm((1024, 1024), BF16), vm((1024, 128), BF16), vm((1024, REST), BF16),
            vm((8, 1024, 512), BF16), vm((8, 512, 1024), BF16),
            vm((4, QT + 8, 128), F32), vm((4, QT + 8, 128), F32), vm((QT, 128), F32), vm((QT, 128), F32),
            vm((4, QT + 16, 128), BF16),
            vm((4, QT + 8, REST), F32), vm((2, QT + 8, REST), F32), vm((128, REST), F32), vm((QT - 120, REST), F32),
            vm((2, 16, 40, 128), F32), vm((16, 40, 128), F32), vm((16, 48, 128), BF16), vm((16, 48, 128), BF16),
            vm((128, 128), F32), vm((16, 2, 32, 128), BF16),
            vm((4, 32, 512), BF16), vm((4, 32, 512), BF16), vm((32, 512), F32), vm((4, 32, 512), BF16),
            vm((2, 16, 32, 128), F32), vm((16, 32, 128), F32), vm((16, 32, 128), BF16), vm((16, 32, 128), BF16),
            vm((16, 2, 32, 128), BF16), vm((4, QT, 128), BF16),
            dma((16,)), dma((12, 4)), dma((12, 4)), dma((5,)), dma((5,)),
            dma((4, 16)), dma((4, 16)), dma((4, 16)), dma((4, 16)),
        ],
        compiler_params=pltpu.CompilerParams(
            collective_id=0, has_side_effects=True, vmem_limit_bytes=53 * 2**20
        ),
    )(tokens, slot_param, scale, w_in, w_out)
    return pl.pallas_call(
        mix,
        name="mix",
        out_shape=jax.ShapeDtypeStruct((1024, 1024), BF16),
        in_specs=[anyspec, anyspec],
        out_specs=anyspec,
        scratch_shapes=[
            vm((4, QT, 128), BF16), vm((16, 2, 32, 128), BF16), vm((128, 1024), BF16), vm((1024, 1024), BF16), dma((9,)),
        ],
        compiler_params=pltpu.CompilerParams(vmem_limit_bytes=16 * 2**20),
    )(comb, slot_out)


def solution(mesh):
    in_specs = (
        P("seq", "width"),
        P("width", None),
        P(),
        P(None, "width", "seq"),
        P(None, "seq", "width"),
    )
    return jax.shard_map(
        per_device, mesh=mesh, in_specs=in_specs, out_specs=P("seq", "width"), check_vma=False
    )
```

```python
import jax
import jax.numpy as jnp
from jax import lax
from jax.experimental import pallas as pl
from jax.experimental.pallas import tpu as pltpu
from jax.sharding import PartitionSpec as P

SLOT_PER = 16
E_RUN = 8
WINDOW = 128
EPS = 1e-06
F32 = jnp.float32
BF16 = jnp.bfloat16
MESH = pl.DeviceIdType.MESH
QT = 256
REST = 896
CHIPS = 16
SENDS = (2, 1, 3)
ARRIVALS = (0, 1, 3, 2)
GROUPS = (0, 1, 3, 2)


def hops(j):
    return (0, 1, 2, 1)[j // 4] + (0, 1, 2, 1)[j % 4]


AXIS = (8, 2, 4, 12, 1, 3)
OTHERS = sorted(range(1, CHIPS), key=lambda j: -hops(j))


def column(row):
    return jnp.transpose(jnp.broadcast_to(row, (128, 128)))


def kernel(
    tok_h, sp_h, scale_h, win_h, wout_h,
    comb_o, so_o,
    scale_ref, tok, spw, spn, win, wout,
    wsend, wrecv, lw, rnv, dsp, nsend, nrecv, relay_a, relay_b,
    wb, pr, ab, rb, gs, si,
    hp, hr, h_own, hb, ob, po, ab2, ro, so, cb,
    ready, ld_sem, x_send, x_recv, c_send, c_recv, s_send, s_recv, f_send, f_recv,
):
    s = lax.axis_index("seq")
    x = lax.axis_index("width")
    c = lax.rem(s, 2)
    p = lax.div(s, 2)
    z = lax.div(p, 4)
    y = lax.rem(p, 4)
    peer = (s + 1 - 2 * c, x)

    def xdev(d):
        return (s, lax.rem(x + d, 4))

    def chip_of(j):
        return lax.rem(z + j // 4, 4) * 4 + lax.rem(y + j % 4, 4)

    def chip_from(j):
        return lax.rem(z + 4 - j // 4, 4) * 4 + lax.rem(y + 4 - j % 4, 4)

    pending, bulk = [], []

    def remote(src, dst, send, recv, to):
        cp = pltpu.make_async_remote_copy(
            src_ref=src, dst_ref=dst, send_sem=send, recv_sem=recv, device_id=to, device_id_type=MESH
        )
        cp.start()
        pending.append((None, cp))
        return cp

    def remote_if(cond, src, dst, send, recv, to):
        cp = pltpu.make_async_remote_copy(
            src_ref=src, dst_ref=dst, send_sem=send, recv_sem=recv, device_id=to, device_id_type=MESH
        )
        pl.when(cond)(cp.start)
        pending.append((cond, cp))
        return cp

    def sent(copies):
        for cp in copies:
            for k, (cond, other) in enumerate(pending):
                if other is cp:
                    del pending[k]
                    break
            if cond is None:
                cp.wait_send()
            else:
                pl.when(cond)(cp.wait_send)

    def drain(count):
        for cond, cp in pending[:count]:
            if cond is None:
                cp.wait_send()
            else:
                pl.when(cond)(cp.wait_send)
        del pending[:count]

    xn = []

    def piece(d, start, count, k):
        rows, slot = pl.ds(start, count), d // 2
        xn.append(remote(nsend.at[d, rows], nrecv.at[slot, rows], x_send.at[k, slot], x_recv.at[k, slot], xdev(d)))
        bulk.append(pending.pop())

    def arrival(dst, send, recv):
        return pltpu.make_async_remote_copy(
            src_ref=dst, dst_ref=dst, send_sem=send, recv_sem=recv, device_id=peer, device_id_type=MESH
        )

    barrier = pltpu.get_barrier_semaphore()
    for j in AXIS:
        pl.semaphore_signal(barrier, inc=1, device_id=(chip_of(j) * 2 + c, x), device_id_type=MESH)
    for d in SENDS:
        pl.semaphore_signal(barrier, inc=1, device_id=xdev(d), device_id_type=MESH)
    pl.semaphore_signal(barrier, inc=1, device_id=peer, device_id_type=MESH)

    def load(src, dst, i):
        cp = pltpu.make_async_copy(src, dst, ld_sem.at[i])
        cp.start()
        return cp

    ld_scale = load(scale_h, scale_ref, 16)
    ld_spw = load(sp_h.at[:, pl.ds(0, WINDOW)], spw, 0)
    ld_tok = {}
    for i, d in enumerate((2, 1, 3, 0)):
        rows = pl.ds(lax.rem(x + d, 4) * QT, QT)
        ld_tok[d] = load(tok_h.at[rows], tok.at[rows], 1 + i)
    ld_spn = load(sp_h.at[:, pl.ds(WINDOW, REST)], spn, 5)
    ld_spw.wait()
    spf = spw[...].astype(F32)
    csq = jnp.sum(spf * spf, axis=0, keepdims=True)
    xw = {}
    for d in (2, 1, 3, 0):
        ld_tok[d].wait()
        t = tok[pl.ds(lax.rem(x + d, 4) * QT, QT), :]
        wsend[d, 0:QT, :] = jnp.dot(t, spw[...], preferred_element_type=F32)
        part = jnp.zeros((QT, 128), F32)
        for b in range(8):
            tf = t[:, b * 128:(b + 1) * 128].astype(F32)
            part = part + tf * tf
        rows = [jnp.sum(jnp.transpose(part[h * 128:(h + 1) * 128]), axis=0, keepdims=True) for h in range(2)]
        wsend[d, QT:QT + 8, :] = jnp.concatenate(rows + [csq, jnp.zeros((5, 128), F32)], axis=0)
        if d == 2:
            pl.semaphore_wait(barrier, 4 + len(AXIS))
        if d:
            xw[d] = remote(wsend.at[d], wrecv.at[d], x_send.at[0, d], x_recv.at[0, d], xdev(d))
    for j in (8, 4, 12):
        pl.semaphore_signal(ready, inc=1, device_id=(chip_of(j) * 2 + c, x), device_id_type=MESH)

    ld_win = {}
    for i, dz in enumerate(GROUPS):
        e = 2 * lax.rem(z + 4 - dz, 4)
        ld_win[dz] = load(win_h.at[pl.ds(e, 2)], win.at[pl.ds(e, 2)], 6 + i)
    ld_wout = {}
    for i, d in enumerate(ARRIVALS):
        e = 2 * lax.rem(x + 4 - d, 4)
        ld_wout[d] = load(wout_h.at[pl.ds(e, 2)], wout.at[pl.ds(e, 2)], 10 + i)

    ld_spn.wait()
    csn = jnp.zeros((8, REST), F32)
    for b in range(32):
        sf = spn[b * 32:(b + 1) * 32, :].astype(F32)
        sq = sf * sf
        csn = csn + sq[0:8] + sq[8:16] + sq[16:24] + sq[24:32]
    for d in (2, 1, 3, 0):
        t = tok[pl.ds(lax.rem(x + d, 4) * QT, QT), :]
        nsend[d, 0:QT, :] = jnp.dot(t, spn[...], preferred_element_type=F32)
        nsend[d, QT:QT + 8, :] = csn

    sent(list(xw.values()))
    piece(1, 128, 32, 6)
    piece(3, 0, 32, 6)
    tot = wsend[0]
    for d in (1, 3, 2):
        xw[d].wait_recv()
        tot = tot + wrecv[d]
    rn = jnp.sqrt(jnp.concatenate([column(tot[QT:QT + 1]), column(tot[QT + 1:QT + 2])], axis=0) + EPS)
    cn = jnp.sqrt(tot[QT + 2:QT + 3] + EPS)
    ld_scale.wait()
    scale = scale_ref[0]
    logits = scale * tot[0:QT] / (rn * cn)
    lw[...] = logits
    rnv[...] = rn
    m = jnp.max(logits, axis=0, keepdims=True).astype(BF16)
    dsp[x, 0:QT, :] = jnp.exp(logits - m.astype(F32)).astype(BF16)
    dsp[x, QT:QT + 16, :] = jnp.broadcast_to(m, (16, 128))
    xd = {d: remote(dsp.at[x], dsp.at[x], x_send.at[1, d], x_recv.at[1, d], xdev(d)) for d in SENDS}

    sent(list(xd.values()))
    piece(1, 160, 32, 7)
    piece(3, 32, 32, 7)
    for d in SENDS:
        xd[d].wait_recv()
    via_a = remote(nsend.at[2, pl.ds(0, 128)], relay_a, x_send.at[2, 0], x_recv.at[2, 0], xdev(1))
    via_b = remote(nsend.at[2, pl.ds(128, 136)], relay_b, x_send.at[2, 1], x_recv.at[2, 1], xdev(3))
    bulk.extend((pending.pop(), pending.pop()))
    ms = [dsp[q, QT:QT + 1, :].astype(F32) for q in range(4)]
    mseq = jnp.maximum(jnp.maximum(ms[0], ms[1]), jnp.maximum(ms[2], ms[3]))
    total = jnp.zeros((1, 128), F32)
    cols = []
    for q in range(4):
        f = jnp.exp(ms[q] - mseq)
        total = total + f * jnp.sum(dsp[q, 0:QT, :].astype(F32), axis=0, keepdims=True)
        cols.append(column(f))
    stats = jnp.concatenate([mseq, total, jnp.zeros((6, 128), F32)], axis=0)
    cw = None
    for k in (1 - c, c):
        for h in range(2):
            at = pl.multiple_of(h * 512 + k * 256, 256)
            acc = jnp.zeros((128, 256), F32)
            for q in range(4):
                prod = lax.dot_general(
                    dsp[q, 0:QT, :], tok[q * QT:(q + 1) * QT, pl.ds(at, 256)],
                    (((0,), (0,)), ((), ())), preferred_element_type=F32,
                )
                acc = acc + prod * jnp.concatenate([cols[q], cols[q]], axis=1)
            for e in range(E_RUN):
                for b in range(2):
                    wb[k, e * 2 + h, b * 16:(b + 1) * 16, :] = acc[e * 16:(e + 1) * 16, b * 128:(b + 1) * 128]
                wb[k, e * 2 + h, 32:40, :] = stats
        if cw is None:
            cw = remote(wb.at[1 - c], pr, c_send.at[0], c_recv.at[0], peer)

    cw.wait_recv()
    m_a, m_b = wb[c, 0, 32:33, :], pr[0, 32:33, :]
    m2 = jnp.maximum(m_a, m_b)
    f_a, f_b = jnp.exp(m_a - m2), jnp.exp(m_b - m2)
    t2 = f_a * wb[c, 0, 33:34, :] + f_b * pr[0, 33:34, :]
    t_hi = t2.astype(BF16).astype(F32)
    stats = jnp.concatenate([m2, t_hi, t2 - t_hi, jnp.zeros((13, 128), F32)], axis=0).astype(BF16)
    c_a, c_b = column(f_a), column(f_b)
    for i in range(CHIPS):
        e = i // 2
        k_a, k_b = c_a[e * 16:(e + 1) * 16], c_b[e * 16:(e + 1) * 16]
        for b in range(2):
            r = slice(b * 16, (b + 1) * 16)
            ab[i, r, :] = (wb[c, i, r, :] * k_a + pr[i, r, :] * k_b).astype(BF16)
        ab[i, 32:48, :] = stats
    pl.semaphore_wait(ready, 3)
    sw = {
        j: remote(ab.at[chip_of(j)], rb.at[j], s_send.at[0, j], s_recv.at[0, j], (chip_of(j) * 2 + c, x))
        for j in OTHERS
    }
    drain(len(pending) - 15)
    for j in range(1, CHIPS):
        sw[j].wait_recv()
    piece(1, 192, 72, 8)
    piece(3, 64, 64, 8)
    st = [ab[p, 32:48, :].astype(F32)] + [rb[j, 32:48, :].astype(F32) for j in range(1, CHIPS)]
    mr = [v[0:1] for v in st]
    tr = [v[1:2] + v[2:3] for v in st]
    top = mr[0]
    for v in mr[1:]:
        top = jnp.maximum(top, v)
    fr = [jnp.exp(v - top) for v in mr]
    total = fr[0] * tr[0]
    for f, t in zip(fr[1:], tr[1:]):
        total = total + f * t
    gs[...] = jnp.transpose(jnp.concatenate([f / total for f in fr] + [jnp.zeros((112, 128), F32)], axis=0))
    ge = gs[pl.ds(lax.div(p, 2) * 16, 16), :]
    acc = [jnp.zeros((16, 128), F32)] * 2
    for j in range(CHIPS):
        w = ge[:, j:j + 1]
        for b in range(2):
            r = slice(b * 16, (b + 1) * 16)
            v = ab[p, r, :] if j == 0 else rb[j, r, :]
            acc[b] = acc[b] + v.astype(F32) * w
    si[p, c, :, :] = jnp.concatenate(acc, axis=0).astype(BF16)


    def gather(buf, k):
        out, other = {}, {}
        for j in OTHERS:
            to = (chip_of(j) * 2 + c, x)
            out[j] = remote(buf.at[p, c], buf.at[p, c], s_send.at[k, j], s_recv.at[k, j], to)
        other[0] = remote(buf.at[p, c], buf.at[p, c], f_send.at[k, 0], f_recv.at[k, 0], peer)

        def arrive(dz):
            for j in range(dz * 4, dz * 4 + 4):
                if j:
                    out[j].wait_recv()
                    at = chip_from(j)
                    other[j] = remote(buf.at[at, c], buf.at[at, c], f_send.at[k, j], f_recv.at[k, j], peer)

        def whole(dz):
            for j in range(dz * 4, dz * 4 + 4):
                other[j].wait_recv()

        return arrive, whole

    count = len(pending)
    arrive, whole = gather(si, 1)
    drain(count)
    count = len(pending)

    xp = []
    arrive(GROUPS[0])
    for i, dz in enumerate(GROUPS):
        if i < 3:
            arrive(GROUPS[i + 1])
        whole(dz)
        q = lax.rem(z + 4 - dz, 4)
        d = lax.rem(q + 4 - x, 4)
        ld_win[dz].wait()
        own = []
        for k in range(2):
            e = 2 * q + k
            rows = jnp.concatenate(
                [si[e * 2 + h, g, b * 16:(b + 1) * 16, :] for h in range(2) for g in range(2) for b in range(2)],
                axis=1,
            )
            own.append(jnp.dot(rows, win[e], preferred_element_type=F32))
        own = jnp.concatenate(own, axis=0)
        hp[dz] = own.astype(BF16)
        xp.append(remote_if(d != 0, hp.at[dz], hr.at[d], x_send.at[3, dz], x_recv.at[3, d], (s, q)))

        @pl.when(d == 0)
        def _(own=own):
            h_own[...] = own

    drain(count)
    xh = {d: arrival(hr.at[d], x_send.at[3, 0], x_recv.at[3, d]) for d in (1, 2, 3)}
    via_a.wait_recv()
    nsend[1, 0:128, :] = nsend[1, 0:128, :] + relay_a[...]
    via_b.wait_recv()
    nsend[3, 128:264, :] = nsend[3, 128:264, :] + relay_b[...]
    sent(xp)
    piece(1, 0, 32, 9)
    piece(3, 128, 32, 9)
    hidden = h_own[...]
    for d in (1, 3, 2):
        xh[d].wait_recv()
        hidden = hidden + hr[d].astype(F32)
    hidden = 0.5 * hidden * (1.0 + lax.erf(hidden * 0.7071067811865476))
    hb[x] = hidden.astype(BF16)
    xg = {d: remote(hb.at[x], hb.at[x], x_send.at[4, d], x_recv.at[4, d], xdev(d)) for d in SENDS}

    drain(len(pending) - 3)
    sent(list(xg.values()))
    piece(1, 32, 96, 10)
    piece(3, 160, 104, 10)
    def chips_sum(q, copy):
        copy.wait_recv()
        block = pl.ds(4 * q, 4)
        ab2[block] = (ob[c, block] + po[block]).astype(BF16)
        dz = lax.rem(q + 4 - z, 4)
        for dy in range(4):
            to = q * 4 + lax.rem(y + dy, 4)
            j = dz * 4 + dy
            args = (ab2.at[to], ro.at[j], s_send.at[2, j], s_recv.at[2, j], (to * 2 + c, x))
            if dy:
                remote(*args)
            else:
                remote_if(dz != 0, *args)

    count = len(pending)
    last = None
    for i, d in enumerate(ARRIVALS):
        q = lax.rem(x + 4 - d, 4)
        if d:
            xg[d].wait_recv()
        ld_wout[d].wait()
        for k in range(2):
            e = 2 * q + k
            o = jnp.dot(hb[q, k * 16:(k + 1) * 16, :], wout[e], preferred_element_type=F32)
            for h in range(2):
                for g in range(2):
                    for b in range(2):
                        at = h * 512 + g * 256 + b * 128
                        ob[g, e * 2 + h, b * 16:(b + 1) * 16, :] = o[:, at:at + 128]
        block = pl.ds(4 * q, 4)
        copy = remote(ob.at[1 - c, block], po.at[block], c_send.at[1 + i], c_recv.at[1 + i], peer)
        if last is not None:
            chips_sum(*last)
        last = (q, copy)
    chips_sum(*last)
    drain(count)
    sv = {j: arrival(ro.at[j], s_send.at[2, 0], s_recv.at[2, j]) for j in range(1, CHIPS)}
    for j in range(1, CHIPS):
        sv[j].wait_recv()
    acc = ab2[p].astype(F32)
    for j in range(1, CHIPS):
        acc = acc + ro[j].astype(F32)
    so[p, c, :, :] = acc.astype(BF16)
    count = len(pending)
    arrive, whole = gather(so, 3)
    drain(count)

    for cp in xn:
        cp.wait_recv()
    cs = nsend[0, QT:QT + 8, :] + nrecv[0, QT:QT + 8, :] + nrecv[1, QT:QT + 8, :]
    cnn = jnp.sqrt(jnp.sum(cs, axis=0, keepdims=True) + EPS)
    for g in range(4):
        r = slice(g * 64, (g + 1) * 64)
        rg = rnv[r, :]
        lwin = lw[r, :]
        ls = []
        top = lwin
        for b in range(7):
            at = slice(b * 128, (b + 1) * 128)
            raw = nsend[0, r, at] + nrecv[0, r, at] + nrecv[1, r, at]
            lg = scale * raw / (rg * cnn[:, at])
            ls.append(lg)
            top = jnp.maximum(top, lg)
        tmax = jnp.max(top, axis=1, keepdims=True)
        ew = jnp.exp(lwin - tmax)
        tsum = ew
        for lg in ls:
            tsum = tsum + jnp.exp(lg - tmax)
        ttot = jnp.sum(tsum, axis=1, keepdims=True)
        cb[x, r, :] = (ew / ttot).astype(BF16)
    xc = {d: remote(cb.at[x], cb.at[x], x_send.at[5, d], x_recv.at[5, d], xdev(d)) for d in SENDS}

    for dz in GROUPS:
        arrive(dz)
    for d in SENDS:
        xc[d].wait_recv()
    store_comb = load(cb, comb_o, 14)
    for dz in GROUPS:
        whole(dz)
    load(so, so_o, 15).wait()
    store_comb.wait()
    for cond, cp in pending + bulk:
        if cond is None:
            cp.wait_send()
        else:
            pl.when(cond)(cp.wait_send)


def mix(comb, so, out_h, slot_out, out, sem):
    def copy(src, dst, i):
        cp = pltpu.make_async_copy(src, dst, sem.at[i])
        cp.start()
        return cp

    for e in range(E_RUN):
        for h in range(2):
            for g in range(2):
                for b in range(2):
                    at = h * 512 + g * 256 + b * 128
                    slot_out[e * 16:(e + 1) * 16, at:at + 128] = so[e * 2 + h, g, b * 16:(b + 1) * 16, :]
    stores = []
    for g in range(4):
        r = pl.ds(g * QT, QT)
        out[r, :] = jnp.dot(comb[g], slot_out[...], preferred_element_type=F32).astype(BF16)
        stores.append(copy(out.at[r], out_h.at[r], g))
    for cp in stores:
        cp.wait()


def per_device(tokens, slot_param, scale, w_in, w_out):
    vm = pltpu.VMEM
    dma = pltpu.SemaphoreType.DMA
    anyspec = pl.BlockSpec(memory_space=pl.ANY)
    comb, slot_out = pl.pallas_call(
        kernel,
        name="moe_exchange",
        out_shape=(jax.ShapeDtypeStruct((4, QT, 128), BF16), jax.ShapeDtypeStruct((16, 2, 32, 128), BF16)),
        in_specs=[anyspec, anyspec, anyspec, anyspec, anyspec],
        out_specs=(anyspec, anyspec),
        scratch_shapes=[
            pltpu.SMEM((1,), F32), vm((1024, 1024), BF16), vm((1024, 128), BF16), vm((1024, REST), BF16),
            vm((8, 1024, 512), BF16), vm((8, 512, 1024), BF16),
            vm((4, QT + 8, 128), F32), vm((4, QT + 8, 128), F32), vm((QT, 128), F32), vm((QT, 128), F32),
            vm((4, QT + 16, 128), BF16),
            vm((4, QT + 8, REST), F32), vm((2, QT + 8, REST), F32), vm((128, REST), F32), vm((QT - 120, REST), F32),
            vm((2, 16, 40, 128), F32), vm((16, 40, 128), F32), vm((16, 48, 128), BF16), vm((16, 48, 128), BF16),
            vm((128, 128), F32), vm((16, 2, 32, 128), BF16),
            vm((4, 32, 512), BF16), vm((4, 32, 512), BF16), vm((32, 512), F32), vm((4, 32, 512), BF16),
            vm((2, 16, 32, 128), F32), vm((16, 32, 128), F32), vm((16, 32, 128), BF16), vm((16, 32, 128), BF16),
            vm((16, 2, 32, 128), BF16), vm((4, QT, 128), BF16),
            pltpu.SemaphoreType.REGULAR, dma((17,)), dma((12, 4)), dma((12, 4)), dma((5,)), dma((5,)),
            dma((4, 16)), dma((4, 16)), dma((4, 16)), dma((4, 16)),
        ],
        compiler_params=pltpu.CompilerParams(
            collective_id=0, has_side_effects=True, vmem_limit_bytes=53 * 2**20
        ),
    )(tokens, slot_param, scale, w_in, w_out)
    return pl.pallas_call(
        mix,
        name="mix",
        out_shape=jax.ShapeDtypeStruct((1024, 1024), BF16),
        in_specs=[pl.BlockSpec(memory_space=pltpu.VMEM)] * 2,
        out_specs=anyspec,
        scratch_shapes=[vm((128, 1024), BF16), vm((1024, 1024), BF16), dma((4,))],
        compiler_params=pltpu.CompilerParams(vmem_limit_bytes=16 * 2**20),
    )(comb, slot_out)


def solution(mesh):
    in_specs = (
        P("seq", "width"),
        P("width", None),
        P(),
        P(None, "width", "seq"),
        P(None, "seq", "width"),
    )
    return jax.shard_map(
        per_device, mesh=mesh, in_specs=in_specs, out_specs=P("seq", "width"), check_vma=False
    )
```

```python
import jax
import jax.numpy as jnp
from jax import lax
from jax.experimental import pallas as pl
from jax.experimental.pallas import tpu as pltpu
from jax.sharding import PartitionSpec as P

SLOT_PER = 16
E_RUN = 8
WINDOW = 128
EPS = 1e-06
F32 = jnp.float32
BF16 = jnp.bfloat16
MESH = pl.DeviceIdType.MESH
QT = 256
REST = 896
CHIPS = 16
SENDS = (2, 1, 3)
ARRIVALS = (0, 1, 3, 2)
GROUPS = (0, 1, 3, 2)


def hops(j):
    return (0, 1, 2, 1)[j // 4] + (0, 1, 2, 1)[j % 4]


AXIS = (8, 2, 4, 12, 1, 3)
OTHERS = sorted(range(1, CHIPS), key=lambda j: -hops(j))


def column(row):
    return jnp.transpose(jnp.broadcast_to(row, (128, 128)))


def kernel(
    tok_h, sp_h, scale_h, win_h, wout_h,
    comb_o, so_o,
    scale_ref, tok, spw, spn, win, wout,
    wsend, wrecv, lw, rnv, dsp, cq, nsend, nrecv, relay_a, relay_b,
    wb, pr, ab, rb, gs, si,
    hp, hr, h_own, h_half, hb, ob, po, ab2, ro, so, cb,
    ready, ld_sem, x_send, x_recv, c_send, c_recv, s_send, s_recv, f_send, f_recv,
):
    s = lax.axis_index("seq")
    x = lax.axis_index("width")
    c = lax.rem(s, 2)
    p = lax.div(s, 2)
    z = lax.div(p, 4)
    y = lax.rem(p, 4)
    peer = (s + 1 - 2 * c, x)

    def xdev(d):
        return (s, lax.rem(x + d, 4))

    def chip_of(j):
        return lax.rem(z + j // 4, 4) * 4 + lax.rem(y + j % 4, 4)

    def chip_from(j):
        return lax.rem(z + 4 - j // 4, 4) * 4 + lax.rem(y + 4 - j % 4, 4)

    pending, bulk = [], []

    def remote(src, dst, send, recv, to):
        cp = pltpu.make_async_remote_copy(
            src_ref=src, dst_ref=dst, send_sem=send, recv_sem=recv, device_id=to, device_id_type=MESH
        )
        cp.start()
        pending.append((None, cp))
        return cp

    def remote_if(cond, src, dst, send, recv, to):
        cp = pltpu.make_async_remote_copy(
            src_ref=src, dst_ref=dst, send_sem=send, recv_sem=recv, device_id=to, device_id_type=MESH
        )
        pl.when(cond)(cp.start)
        pending.append((cond, cp))
        return cp

    def sent(copies):
        for cp in copies:
            for k, (cond, other) in enumerate(pending):
                if other is cp:
                    del pending[k]
                    break
            if cond is None:
                cp.wait_send()
            else:
                pl.when(cond)(cp.wait_send)

    def drain(count):
        for cond, cp in pending[:count]:
            if cond is None:
                cp.wait_send()
            else:
                pl.when(cond)(cp.wait_send)
        del pending[:count]

    xn = []

    def piece(d, start, count, k):
        rows, slot = pl.ds(start, count), d // 2
        xn.append(remote(nsend.at[d, rows], nrecv.at[slot, rows], x_send.at[k, slot], x_recv.at[k, slot], xdev(d)))
        bulk.append(pending.pop())

    def arrival(dst, send, recv):
        return pltpu.make_async_remote_copy(
            src_ref=dst, dst_ref=dst, send_sem=send, recv_sem=recv, device_id=peer, device_id_type=MESH
        )

    barrier = pltpu.get_barrier_semaphore()
    for j in AXIS:
        pl.semaphore_signal(barrier, inc=1, device_id=(chip_of(j) * 2 + c, x), device_id_type=MESH)
    for d in SENDS:
        pl.semaphore_signal(barrier, inc=1, device_id=xdev(d), device_id_type=MESH)
    pl.semaphore_signal(barrier, inc=1, device_id=peer, device_id_type=MESH)

    def load(src, dst, i):
        cp = pltpu.make_async_copy(src, dst, ld_sem.at[i])
        cp.start()
        return cp

    ld_scale = load(scale_h, scale_ref, 16)
    ld_spw = load(sp_h.at[:, pl.ds(0, WINDOW)], spw, 0)
    ld_tok = {}
    for i, d in enumerate((2, 1, 3, 0)):
        rows = pl.ds(lax.rem(x + d, 4) * QT, QT)
        ld_tok[d] = load(tok_h.at[rows], tok.at[rows], 1 + i)
    ld_spn = load(sp_h.at[:, pl.ds(WINDOW, REST)], spn, 5)
    ld_spw.wait()
    spf = spw[...].astype(F32)
    csq = jnp.sum(spf * spf, axis=0, keepdims=True)
    xw = {}
    for d in (2, 1, 3, 0):
        ld_tok[d].wait()
        t = tok[pl.ds(lax.rem(x + d, 4) * QT, QT), :]
        wsend[d, 0:QT, :] = jnp.dot(t, spw[...], preferred_element_type=F32)
        part = jnp.zeros((QT, 128), F32)
        for b in range(8):
            tf = t[:, b * 128:(b + 1) * 128].astype(F32)
            part = part + tf * tf
        rows = [jnp.sum(jnp.transpose(part[h * 128:(h + 1) * 128]), axis=0, keepdims=True) for h in range(2)]
        wsend[d, QT:QT + 8, :] = jnp.concatenate(rows + [csq, jnp.zeros((5, 128), F32)], axis=0)
        if d == 2:
            pl.semaphore_wait(barrier, 4 + len(AXIS))
        if d:
            xw[d] = remote(wsend.at[d], wrecv.at[d], x_send.at[0, d], x_recv.at[0, d], xdev(d))
    for j in (8, 4, 12):
        pl.semaphore_signal(ready, inc=1, device_id=(chip_of(j) * 2 + c, x), device_id_type=MESH)

    ld_win = {}
    for i, dz in enumerate(GROUPS):
        e = 2 * lax.rem(z + 4 - dz, 4)
        ld_win[dz] = load(win_h.at[pl.ds(e, 2)], win.at[pl.ds(e, 2)], 6 + i)
    ld_wout = {}
    for i, d in enumerate(ARRIVALS):
        e = 2 * lax.rem(x + 4 - d, 4)
        ld_wout[d] = load(wout_h.at[pl.ds(e, 2)], wout.at[pl.ds(e, 2)], 10 + i)

    ld_spn.wait()
    csn = jnp.zeros((8, REST), F32)
    for b in range(32):
        sf = spn[b * 32:(b + 1) * 32, :].astype(F32)
        sq = sf * sf
        csn = csn + sq[0:8] + sq[8:16] + sq[16:24] + sq[24:32]
    csr = jnp.sum(csn, axis=0, keepdims=True)
    cq[0] = jnp.concatenate([csr[:, b * 128:(b + 1) * 128] for b in range(7)] + [jnp.ones((1, 128), F32)], axis=0)
    xq = {d: remote(cq.at[0], cq.at[d], x_send.at[11, d], x_recv.at[11, d], xdev(d)) for d in SENDS}
    for d in (2, 1, 3, 0):
        t = tok[pl.ds(lax.rem(x + d, 4) * QT, QT), :]
        nsend[d, 0:QT, :] = jnp.dot(t, spn[...], preferred_element_type=F32)

    sent(list(xw.values()))
    piece(1, 128, 40, 6)
    piece(3, 0, 40, 6)
    tot = wsend[0]
    for d in (1, 3, 2):
        xw[d].wait_recv()
        tot = tot + wrecv[d]
    rn = jnp.sqrt(jnp.concatenate([column(tot[QT:QT + 1]), column(tot[QT + 1:QT + 2])], axis=0) + EPS)
    cn = jnp.sqrt(tot[QT + 2:QT + 3] + EPS)
    ld_scale.wait()
    scale = scale_ref[0]
    logits = scale * tot[0:QT] / (rn * cn)
    lw[...] = logits
    rnv[...] = rn
    m = jnp.max(logits, axis=0, keepdims=True).astype(BF16)
    dsp[x, 0:QT, :] = jnp.exp(logits - m.astype(F32)).astype(BF16)
    dsp[x, QT:QT + 16, :] = jnp.broadcast_to(m, (16, 128))
    xd = {d: remote(dsp.at[x], dsp.at[x], x_send.at[1, d], x_recv.at[1, d], xdev(d)) for d in SENDS}

    sent(list(xd.values()))
    piece(1, 168, 32, 7)
    piece(3, 40, 32, 7)
    for d in SENDS:
        xd[d].wait_recv()
    via_a = remote(nsend.at[2, pl.ds(0, 128)], relay_a, x_send.at[2, 0], x_recv.at[2, 0], xdev(1))
    via_b = remote(nsend.at[2, pl.ds(128, 128)], relay_b, x_send.at[2, 1], x_recv.at[2, 1], xdev(3))
    bulk.extend((pending.pop(), pending.pop()))
    ms = [dsp[q, QT:QT + 1, :].astype(F32) for q in range(4)]
    mseq = jnp.maximum(jnp.maximum(ms[0], ms[1]), jnp.maximum(ms[2], ms[3]))
    total = jnp.zeros((1, 128), F32)
    cols = []
    for q in range(4):
        f = jnp.exp(ms[q] - mseq)
        total = total + f * jnp.sum(dsp[q, 0:QT, :].astype(F32), axis=0, keepdims=True)
        cols.append(column(f))
    stats = jnp.concatenate([mseq, total, jnp.zeros((6, 128), F32)], axis=0)
    cw = None
    for k in (1 - c, c):
        for h in range(2):
            at = pl.multiple_of(h * 512 + k * 256, 256)
            acc = jnp.zeros((128, 256), F32)
            for q in range(4):
                prod = lax.dot_general(
                    dsp[q, 0:QT, :], tok[q * QT:(q + 1) * QT, pl.ds(at, 256)],
                    (((0,), (0,)), ((), ())), preferred_element_type=F32,
                )
                acc = acc + prod * jnp.concatenate([cols[q], cols[q]], axis=1)
            for e in range(E_RUN):
                for b in range(2):
                    wb[k, e * 2 + h, b * 16:(b + 1) * 16, :] = acc[e * 16:(e + 1) * 16, b * 128:(b + 1) * 128]
                wb[k, e * 2 + h, 32:40, :] = stats
        if cw is None:
            cw = remote(wb.at[1 - c], pr, c_send.at[0], c_recv.at[0], peer)

    cw.wait_recv()
    m_a, m_b = wb[c, 0, 32:33, :], pr[0, 32:33, :]
    m2 = jnp.maximum(m_a, m_b)
    f_a, f_b = jnp.exp(m_a - m2), jnp.exp(m_b - m2)
    t2 = f_a * wb[c, 0, 33:34, :] + f_b * pr[0, 33:34, :]
    t_hi = t2.astype(BF16).astype(F32)
    stats = jnp.concatenate([m2, t_hi, t2 - t_hi, jnp.zeros((13, 128), F32)], axis=0).astype(BF16)
    c_a, c_b = column(f_a), column(f_b)
    for i in range(CHIPS):
        e = i // 2
        k_a, k_b = c_a[e * 16:(e + 1) * 16], c_b[e * 16:(e + 1) * 16]
        for b in range(2):
            r = slice(b * 16, (b + 1) * 16)
            ab[i, r, :] = (wb[c, i, r, :] * k_a + pr[i, r, :] * k_b).astype(BF16)
        ab[i, 32:48, :] = stats
    pl.semaphore_wait(ready, 3)
    sw = {
        j: remote(ab.at[chip_of(j)], rb.at[j], s_send.at[0, j], s_recv.at[0, j], (chip_of(j) * 2 + c, x))
        for j in OTHERS
    }
    drain(len(pending) - 15)
    for j in range(1, CHIPS):
        sw[j].wait_recv()
    piece(1, 200, 40, 8)
    piece(3, 72, 40, 8)
    st = [ab[p, 32:48, :].astype(F32)] + [rb[j, 32:48, :].astype(F32) for j in range(1, CHIPS)]
    mr = [v[0:1] for v in st]
    tr = [v[1:2] + v[2:3] for v in st]
    top = mr[0]
    for v in mr[1:]:
        top = jnp.maximum(top, v)
    fr = [jnp.exp(v - top) for v in mr]
    total = fr[0] * tr[0]
    for f, t in zip(fr[1:], tr[1:]):
        total = total + f * t
    gs[...] = jnp.transpose(jnp.concatenate([f / total for f in fr] + [jnp.zeros((112, 128), F32)], axis=0))
    ge = gs[pl.ds(lax.div(p, 2) * 16, 16), :]
    acc = [jnp.zeros((16, 128), F32)] * 2
    for j in range(CHIPS):
        w = ge[:, j:j + 1]
        for b in range(2):
            r = slice(b * 16, (b + 1) * 16)
            v = ab[p, r, :] if j == 0 else rb[j, r, :]
            acc[b] = acc[b] + v.astype(F32) * w
    si[p, c, :, :] = jnp.concatenate(acc, axis=0).astype(BF16)


    def gather(buf, k):
        out, other = {}, {}
        for j in OTHERS:
            to = (chip_of(j) * 2 + c, x)
            out[j] = remote(buf.at[p, c], buf.at[p, c], s_send.at[k, j], s_recv.at[k, j], to)
        other[0] = remote(buf.at[p, c], buf.at[p, c], f_send.at[k, 0], f_recv.at[k, 0], peer)

        def arrive(dz):
            for j in range(dz * 4, dz * 4 + 4):
                if j:
                    out[j].wait_recv()
                    at = chip_from(j)
                    other[j] = remote(buf.at[at, c], buf.at[at, c], f_send.at[k, j], f_recv.at[k, j], peer)

        def whole(dz):
            for j in range(dz * 4, dz * 4 + 4):
                other[j].wait_recv()

        return arrive, whole

    count = len(pending)
    arrive, whole = gather(si, 1)
    drain(count)
    count = len(pending)

    def half(dz, g):
        parts = []
        for k in range(2):
            e = 2 * lax.rem(z + 4 - dz, 4) + k
            part = jnp.zeros((16, 512), F32)
            for h in range(2):
                rows = jnp.concatenate([si[e * 2 + h, g, 0:16, :], si[e * 2 + h, g, 16:32, :]], axis=1)
                at = pl.multiple_of(h * 512 + g * 256, 256)
                part = part + jnp.dot(rows, win[e, pl.ds(at, 256), :], preferred_element_type=F32)
            parts.append(part)
        return jnp.concatenate(parts, axis=0)

    xp = []
    for dz in GROUPS:
        arrive(dz)
        ld_win[dz].wait()
        h_half[dz] = half(dz, c)
    for dz in GROUPS:
        whole(dz)
        q = lax.rem(z + 4 - dz, 4)
        d = lax.rem(q + 4 - x, 4)
        own = h_half[dz] + half(dz, 1 - c)
        hp[dz] = own.astype(BF16)
        xp.append(remote_if(d != 0, hp.at[dz], hr.at[d], x_send.at[3, dz], x_recv.at[3, d], (s, q)))

        @pl.when(d == 0)
        def _(own=own):
            h_own[...] = own

    drain(count)
    xh = {d: arrival(hr.at[d], x_send.at[3, 0], x_recv.at[3, d]) for d in (1, 2, 3)}
    via_a.wait_recv()
    nsend[1, 0:128, :] = nsend[1, 0:128, :] + relay_a[...]
    via_b.wait_recv()
    nsend[3, 128:256, :] = nsend[3, 128:256, :] + relay_b[...]
    sent(xp)
    piece(1, 0, 32, 9)
    piece(3, 128, 32, 9)
    hidden = h_own[...]
    for d in (1, 3, 2):
        xh[d].wait_recv()
        hidden = hidden + hr[d].astype(F32)
    hidden = 0.5 * hidden * (1.0 + lax.erf(hidden * 0.7071067811865476))
    hb[x] = hidden.astype(BF16)
    xg = {d: remote(hb.at[x], hb.at[x], x_send.at[4, d], x_recv.at[4, d], xdev(d)) for d in SENDS}

    drain(len(pending) - 3)
    sent(list(xg.values()))
    piece(1, 32, 96, 10)
    piece(3, 160, 96, 10)
    piece(1, 240, 16, 12)
    piece(3, 112, 16, 12)
    def chips_sum(q, copy):
        copy.wait_recv()
        block = pl.ds(4 * q, 4)
        ab2[block] = (ob[c, block] + po[block]).astype(BF16)
        dz = lax.rem(q + 4 - z, 4)
        for dy in range(4):
            to = q * 4 + lax.rem(y + dy, 4)
            j = dz * 4 + dy
            args = (ab2.at[to], ro.at[j], s_send.at[2, j], s_recv.at[2, j], (to * 2 + c, x))
            if dy:
                remote(*args)
            else:
                remote_if(dz != 0, *args)

    count = len(pending)
    last = None
    for i, d in enumerate(ARRIVALS):
        q = lax.rem(x + 4 - d, 4)
        if d:
            xg[d].wait_recv()
        ld_wout[d].wait()
        for k in range(2):
            e = 2 * q + k
            o = jnp.dot(hb[q, k * 16:(k + 1) * 16, :], wout[e], preferred_element_type=F32)
            for h in range(2):
                for g in range(2):
                    for b in range(2):
                        at = h * 512 + g * 256 + b * 128
                        ob[g, e * 2 + h, b * 16:(b + 1) * 16, :] = o[:, at:at + 128]
        block = pl.ds(4 * q, 4)
        copy = remote(ob.at[1 - c, block], po.at[block], c_send.at[1 + i], c_recv.at[1 + i], peer)
        if last is not None:
            chips_sum(*last)
        last = (q, copy)
    chips_sum(*last)
    drain(count)
    sv = {j: arrival(ro.at[j], s_send.at[2, 0], s_recv.at[2, j]) for j in range(1, CHIPS)}
    for j in range(1, CHIPS):
        sv[j].wait_recv()
    acc = ab2[p].astype(F32)
    for j in range(1, CHIPS):
        acc = acc + ro[j].astype(F32)
    so[p, c, :, :] = acc.astype(BF16)
    count = len(pending)
    arrive, whole = gather(so, 3)
    drain(count)

    for cp in xn:
        cp.wait_recv()
    for d in SENDS:
        xq[d].wait_recv()
    cnn = jnp.sqrt(cq[0] + cq[1] + cq[2] + cq[3] + EPS)
    for g in range(4):
        r = slice(g * 64, (g + 1) * 64)
        rg = rnv[r, :]
        lwin = lw[r, :]
        ls = []
        top = lwin
        for b in range(7):
            at = slice(b * 128, (b + 1) * 128)
            raw = nsend[0, r, at] + nrecv[0, r, at] + nrecv[1, r, at]
            lg = scale * raw / (rg * cnn[b:b + 1])
            ls.append(lg)
            top = jnp.maximum(top, lg)
        tmax = jnp.max(top, axis=1, keepdims=True)
        ew = jnp.exp(lwin - tmax)
        tsum = ew
        for lg in ls:
            tsum = tsum + jnp.exp(lg - tmax)
        ttot = jnp.sum(tsum, axis=1, keepdims=True)
        cb[x, r, :] = (ew / ttot).astype(BF16)
    xc = {d: remote(cb.at[x], cb.at[x], x_send.at[5, d], x_recv.at[5, d], xdev(d)) for d in SENDS}

    for dz in GROUPS:
        arrive(dz)
    for d in SENDS:
        xc[d].wait_recv()
    store_comb = load(cb, comb_o, 14)
    for dz in GROUPS:
        whole(dz)
    load(so, so_o, 15).wait()
    store_comb.wait()
    for cond, cp in pending + bulk:
        if cond is None:
            cp.wait_send()
        else:
            pl.when(cond)(cp.wait_send)


def mix(comb, so, out_h, slot_out, out, sem):
    def copy(src, dst, i):
        cp = pltpu.make_async_copy(src, dst, sem.at[i])
        cp.start()
        return cp

    for e in range(E_RUN):
        for h in range(2):
            for g in range(2):
                for b in range(2):
                    at = h * 512 + g * 256 + b * 128
                    slot_out[e * 16:(e + 1) * 16, at:at + 128] = so[e * 2 + h, g, b * 16:(b + 1) * 16, :]
    stores = []
    for g in range(4):
        r = pl.ds(g * QT, QT)
        out[r, :] = jnp.dot(comb[g], slot_out[...], preferred_element_type=F32).astype(BF16)
        stores.append(copy(out.at[r], out_h.at[r], g))
    for cp in stores:
        cp.wait()


def per_device(tokens, slot_param, scale, w_in, w_out):
    vm = pltpu.VMEM
    dma = pltpu.SemaphoreType.DMA
    anyspec = pl.BlockSpec(memory_space=pl.ANY)
    comb, slot_out = pl.pallas_call(
        kernel,
        name="moe_exchange",
        out_shape=(jax.ShapeDtypeStruct((4, QT, 128), BF16), jax.ShapeDtypeStruct((16, 2, 32, 128), BF16)),
        in_specs=[anyspec, anyspec, anyspec, anyspec, anyspec],
        out_specs=(anyspec, anyspec),
        scratch_shapes=[
            pltpu.SMEM((1,), F32), vm((1024, 1024), BF16), vm((1024, 128), BF16), vm((1024, REST), BF16),
            vm((8, 1024, 512), BF16), vm((8, 512, 1024), BF16),
            vm((4, QT + 8, 128), F32), vm((4, QT + 8, 128), F32), vm((QT, 128), F32), vm((QT, 128), F32),
            vm((4, QT + 16, 128), BF16),
            vm((4, 8, 128), F32), vm((4, QT, REST), F32), vm((2, QT, REST), F32), vm((128, REST), F32), vm((128, REST), F32),
            vm((2, 16, 40, 128), F32), vm((16, 40, 128), F32), vm((16, 48, 128), BF16), vm((16, 48, 128), BF16),
            vm((128, 128), F32), vm((16, 2, 32, 128), BF16),
            vm((4, 32, 512), BF16), vm((4, 32, 512), BF16), vm((32, 512), F32), vm((4, 32, 512), F32), vm((4, 32, 512), BF16),
            vm((2, 16, 32, 128), F32), vm((16, 32, 128), F32), vm((16, 32, 128), BF16), vm((16, 32, 128), BF16),
            vm((16, 2, 32, 128), BF16), vm((4, QT, 128), BF16),
            pltpu.SemaphoreType.REGULAR, dma((17,)), dma((13, 4)), dma((13, 4)), dma((5,)), dma((5,)),
            dma((4, 16)), dma((4, 16)), dma((4, 16)), dma((4, 16)),
        ],
        compiler_params=pltpu.CompilerParams(
            collective_id=0, has_side_effects=True, vmem_limit_bytes=53 * 2**20
        ),
    )(tokens, slot_param, scale, w_in, w_out)
    return pl.pallas_call(
        mix,
        name="mix",
        out_shape=jax.ShapeDtypeStruct((1024, 1024), BF16),
        in_specs=[pl.BlockSpec(memory_space=pltpu.VMEM)] * 2,
        out_specs=anyspec,
        scratch_shapes=[vm((128, 1024), BF16), vm((1024, 1024), BF16), dma((4,))],
        compiler_params=pltpu.CompilerParams(vmem_limit_bytes=16 * 2**20),
    )(comb, slot_out)


def solution(mesh):
    in_specs = (
        P("seq", "width"),
        P("width", None),
        P(),
        P(None, "width", "seq"),
        P(None, "seq", "width"),
    )
    return jax.shard_map(
        per_device, mesh=mesh, in_specs=in_specs, out_specs=P("seq", "width"), check_vma=False
    )
```

```python
import jax
import jax.numpy as jnp
from jax import lax
from jax.experimental import pallas as pl
from jax.experimental.pallas import tpu as pltpu
from jax.sharding import PartitionSpec as P

SLOT_PER = 16
E_RUN = 8
WINDOW = 128
EPS = 1e-06
F32 = jnp.float32
BF16 = jnp.bfloat16
MESH = pl.DeviceIdType.MESH
QT = 256
REST = 896
CHIPS = 16
SENDS = (2, 1, 3)
ARRIVALS = (0, 1, 3, 2)
GROUPS = (0, 1, 3, 2)


def hops(j):
    return (0, 1, 2, 1)[j // 4] + (0, 1, 2, 1)[j % 4]


AXIS = (8, 2, 4, 12, 1, 3)
OTHERS = sorted(range(1, CHIPS), key=lambda j: -hops(j))


def column(row):
    return jnp.transpose(jnp.broadcast_to(row, (128, 128)))


def kernel(
    tok_h, sp_h, scale_h, win_h, wout_h,
    comb_o, so_o,
    scale_ref, tok, spw, spn, win, wout,
    wsend, wrecv, lw, rnv, dsp, cq, nsend, nrecv, relay_a, relay_b,
    wb, fs, pr, ab, rb, gs, si,
    hp, hr, h_own, h_half, hb, ob, po, ab2, ro, so, cb,
    ready, ld_sem, x_send, x_recv, c_send, c_recv, s_send, s_recv, f_send, f_recv,
):
    s = lax.axis_index("seq")
    x = lax.axis_index("width")
    c = lax.rem(s, 2)
    p = lax.div(s, 2)
    z = lax.div(p, 4)
    y = lax.rem(p, 4)
    peer = (s + 1 - 2 * c, x)

    def xdev(d):
        return (s, lax.rem(x + d, 4))

    def chip_of(j):
        return lax.rem(z + j // 4, 4) * 4 + lax.rem(y + j % 4, 4)

    def chip_from(j):
        return lax.rem(z + 4 - j // 4, 4) * 4 + lax.rem(y + 4 - j % 4, 4)

    pending, bulk = [], []

    def remote(src, dst, send, recv, to):
        cp = pltpu.make_async_remote_copy(
            src_ref=src, dst_ref=dst, send_sem=send, recv_sem=recv, device_id=to, device_id_type=MESH
        )
        cp.start()
        pending.append((None, cp))
        return cp

    def remote_if(cond, src, dst, send, recv, to):
        cp = pltpu.make_async_remote_copy(
            src_ref=src, dst_ref=dst, send_sem=send, recv_sem=recv, device_id=to, device_id_type=MESH
        )
        pl.when(cond)(cp.start)
        pending.append((cond, cp))
        return cp

    def sent(copies):
        for cp in copies:
            for k, (cond, other) in enumerate(pending):
                if other is cp:
                    del pending[k]
                    break
            if cond is None:
                cp.wait_send()
            else:
                pl.when(cond)(cp.wait_send)

    def drain(count):
        for cond, cp in pending[:count]:
            if cond is None:
                cp.wait_send()
            else:
                pl.when(cond)(cp.wait_send)
        del pending[:count]

    xn = []

    def piece(d, start, count, k):
        rows, slot = pl.ds(start, count), d // 2
        xn.append(remote(nsend.at[d, rows], nrecv.at[slot, rows], x_send.at[k, slot], x_recv.at[k, slot], xdev(d)))
        bulk.append(pending.pop())

    def arrival(dst, send, recv):
        return pltpu.make_async_remote_copy(
            src_ref=dst, dst_ref=dst, send_sem=send, recv_sem=recv, device_id=peer, device_id_type=MESH
        )

    barrier = pltpu.get_barrier_semaphore()
    for j in AXIS:
        pl.semaphore_signal(barrier, inc=1, device_id=(chip_of(j) * 2 + c, x), device_id_type=MESH)
    for d in SENDS:
        pl.semaphore_signal(barrier, inc=1, device_id=xdev(d), device_id_type=MESH)
    pl.semaphore_signal(barrier, inc=1, device_id=peer, device_id_type=MESH)

    def load(src, dst, i):
        cp = pltpu.make_async_copy(src, dst, ld_sem.at[i])
        cp.start()
        return cp

    ld_scale = load(scale_h, scale_ref, 16)
    ld_spw = load(sp_h.at[:, pl.ds(0, WINDOW)], spw, 0)
    ld_tok = {}
    for i, d in enumerate((2, 1, 3, 0)):
        rows = pl.ds(lax.rem(x + d, 4) * QT, QT)
        ld_tok[d] = load(tok_h.at[rows], tok.at[rows], 1 + i)
    ld_spn = load(sp_h.at[:, pl.ds(WINDOW, REST)], spn, 5)
    ld_spw.wait()
    spf = spw[...].astype(F32)
    csq = jnp.sum(spf * spf, axis=0, keepdims=True)
    xw = {}
    for d in (2, 1, 3, 0):
        ld_tok[d].wait()
        t = tok[pl.ds(lax.rem(x + d, 4) * QT, QT), :]
        wsend[d, 0:QT, :] = jnp.dot(t, spw[...], preferred_element_type=F32)
        part = jnp.zeros((QT, 128), F32)
        for b in range(8):
            tf = t[:, b * 128:(b + 1) * 128].astype(F32)
            part = part + tf * tf
        rows = [jnp.sum(jnp.transpose(part[h * 128:(h + 1) * 128]), axis=0, keepdims=True) for h in range(2)]
        wsend[d, QT:QT + 8, :] = jnp.concatenate(rows + [csq, jnp.zeros((5, 128), F32)], axis=0)
        if d == 2:
            pl.semaphore_wait(barrier, 4 + len(AXIS))
        if d:
            xw[d] = remote(wsend.at[d], wrecv.at[d], x_send.at[0, d], x_recv.at[0, d], xdev(d))
    for j in (8, 4, 12):
        pl.semaphore_signal(ready, inc=1, device_id=(chip_of(j) * 2 + c, x), device_id_type=MESH)

    ld_win = {}
    for i, dz in enumerate(GROUPS):
        e = 2 * lax.rem(z + 4 - dz, 4)
        ld_win[dz] = load(win_h.at[pl.ds(e, 2)], win.at[pl.ds(e, 2)], 6 + i)
    ld_wout = {}
    for i, d in enumerate(ARRIVALS):
        e = 2 * lax.rem(x + 4 - d, 4)
        ld_wout[d] = load(wout_h.at[pl.ds(e, 2)], wout.at[pl.ds(e, 2)], 10 + i)

    ld_spn.wait()
    csn = jnp.zeros((8, REST), F32)
    for b in range(32):
        sf = spn[b * 32:(b + 1) * 32, :].astype(F32)
        sq = sf * sf
        csn = csn + sq[0:8] + sq[8:16] + sq[16:24] + sq[24:32]
    csr = jnp.sum(csn, axis=0, keepdims=True)
    cq[0] = jnp.concatenate([csr[:, b * 128:(b + 1) * 128] for b in range(7)] + [jnp.ones((1, 128), F32)], axis=0)
    xq = {d: remote(cq.at[0], cq.at[d], x_send.at[11, d], x_recv.at[11, d], xdev(d)) for d in SENDS}
    for d in (2, 1, 3, 0):
        t = tok[pl.ds(lax.rem(x + d, 4) * QT, QT), :]
        nsend[d, 0:QT, :] = jnp.dot(t, spn[...], preferred_element_type=F32)

    sent(list(xw.values()))
    piece(1, 128, 40, 6)
    piece(3, 0, 40, 6)
    tot = wsend[0]
    for d in (1, 3, 2):
        xw[d].wait_recv()
        tot = tot + wrecv[d]
    rn = jnp.sqrt(jnp.concatenate([column(tot[QT:QT + 1]), column(tot[QT + 1:QT + 2])], axis=0) + EPS)
    cn = jnp.sqrt(tot[QT + 2:QT + 3] + EPS)
    ld_scale.wait()
    scale = scale_ref[0]
    logits = scale * tot[0:QT] / (rn * cn)
    lw[...] = logits
    rnv[...] = rn
    m = jnp.max(logits, axis=0, keepdims=True).astype(BF16)
    dsp[x, 0:QT, :] = jnp.exp(logits - m.astype(F32)).astype(BF16)
    dsp[x, QT:QT + 16, :] = jnp.broadcast_to(m, (16, 128))
    xd = {d: remote(dsp.at[x], dsp.at[x], x_send.at[1, d], x_recv.at[1, d], xdev(d)) for d in SENDS}

    sent(list(xd.values()))
    piece(1, 168, 32, 7)
    piece(3, 40, 32, 7)
    for d in SENDS:
        xd[d].wait_recv()
    via_a = remote(nsend.at[2, pl.ds(0, 128)], relay_a, x_send.at[2, 0], x_recv.at[2, 0], xdev(1))
    via_b = remote(nsend.at[2, pl.ds(128, 128)], relay_b, x_send.at[2, 1], x_recv.at[2, 1], xdev(3))
    bulk.extend((pending.pop(), pending.pop()))
    ms = [dsp[q, QT:QT + 1, :].astype(F32) for q in range(4)]
    mseq = jnp.maximum(jnp.maximum(ms[0], ms[1]), jnp.maximum(ms[2], ms[3]))
    total = jnp.zeros((1, 128), F32)
    cols = []
    for q in range(4):
        f = jnp.exp(ms[q] - mseq)
        total = total + f * jnp.sum(dsp[q, 0:QT, :].astype(F32), axis=0, keepdims=True)
        cols.append(column(f))
    stats = jnp.concatenate([mseq, total, jnp.zeros((6, 128), F32)], axis=0)
    cw = None
    for k in (1 - c, c):
        for h in range(2):
            at = pl.multiple_of(h * 512 + k * 256, 256)
            acc = jnp.zeros((128, 256), F32)
            for q in range(4):
                prod = lax.dot_general(
                    dsp[q, 0:QT, :], tok[q * QT:(q + 1) * QT, pl.ds(at, 256)],
                    (((0,), (0,)), ((), ())), preferred_element_type=F32,
                )
                acc = acc + prod * jnp.concatenate([cols[q], cols[q]], axis=1)
            for e in range(E_RUN):
                for b in range(2):
                    wb[k, e * 2 + h, b * 16:(b + 1) * 16, :] = acc[e * 16:(e + 1) * 16, b * 128:(b + 1) * 128]
                wb[k, e * 2 + h, 32:40, :] = stats
        if cw is None:
            cw = remote(wb.at[1 - c], pr, c_send.at[0], c_recv.at[0], peer)

    cw.wait_recv()
    m_a, m_b = wb[c, 0, 32:33, :], pr[0, 32:33, :]
    m2 = jnp.maximum(m_a, m_b)
    f_a, f_b = jnp.exp(m_a - m2), jnp.exp(m_b - m2)
    t2 = f_a * wb[c, 0, 33:34, :] + f_b * pr[0, 33:34, :]
    t_hi = t2.astype(BF16).astype(F32)
    stats = jnp.concatenate([m2, t_hi, t2 - t_hi, jnp.zeros((13, 128), F32)], axis=0).astype(BF16)
    fs[0], fs[1] = column(f_a), column(f_b)
    pl.semaphore_wait(ready, 3)
    sw = {}
    for j in OTHERS + [0]:
        i = chip_of(j)
        rows = pl.ds(lax.div(i, 2) * 16, 16)
        k_a, k_b = fs[0, rows, :], fs[1, rows, :]
        for b in range(2):
            r = slice(b * 16, (b + 1) * 16)
            ab[i, r, :] = (wb[c, i, r, :] * k_a + pr[i, r, :] * k_b).astype(BF16)
        ab[i, 32:48, :] = stats
        if j:
            sw[j] = remote(ab.at[i], rb.at[j], s_send.at[0, j], s_recv.at[0, j], (i * 2 + c, x))
    drain(len(pending) - 15)
    for j in range(1, CHIPS):
        sw[j].wait_recv()
    piece(1, 200, 40, 8)
    piece(3, 72, 40, 8)
    st = [ab[p, 32:48, :].astype(F32)] + [rb[j, 32:48, :].astype(F32) for j in range(1, CHIPS)]
    mr = [v[0:1] for v in st]
    tr = [v[1:2] + v[2:3] for v in st]
    top = mr[0]
    for v in mr[1:]:
        top = jnp.maximum(top, v)
    fr = [jnp.exp(v - top) for v in mr]
    total = fr[0] * tr[0]
    for f, t in zip(fr[1:], tr[1:]):
        total = total + f * t
    gs[...] = jnp.transpose(jnp.concatenate([f / total for f in fr] + [jnp.zeros((112, 128), F32)], axis=0))
    ge = gs[pl.ds(lax.div(p, 2) * 16, 16), :]
    acc = [jnp.zeros((16, 128), F32)] * 2
    for j in range(CHIPS):
        w = ge[:, j:j + 1]
        for b in range(2):
            r = slice(b * 16, (b + 1) * 16)
            v = ab[p, r, :] if j == 0 else rb[j, r, :]
            acc[b] = acc[b] + v.astype(F32) * w
    si[p, c, :, :] = jnp.concatenate(acc, axis=0).astype(BF16)


    def gather(buf, k):
        out, other = {}, {}
        for j in OTHERS:
            to = (chip_of(j) * 2 + c, x)
            out[j] = remote(buf.at[p, c], buf.at[p, c], s_send.at[k, j], s_recv.at[k, j], to)
        other[0] = remote(buf.at[p, c], buf.at[p, c], f_send.at[k, 0], f_recv.at[k, 0], peer)

        def arrive(dz):
            for j in range(dz * 4, dz * 4 + 4):
                if j:
                    out[j].wait_recv()
                    at = chip_from(j)
                    other[j] = remote(buf.at[at, c], buf.at[at, c], f_send.at[k, j], f_recv.at[k, j], peer)

        def whole(dz):
            for j in range(dz * 4, dz * 4 + 4):
                other[j].wait_recv()

        return arrive, whole

    count = len(pending)
    arrive, whole = gather(si, 1)
    drain(count)
    count = len(pending)

    def half(dz, g):
        parts = []
        for k in range(2):
            e = 2 * lax.rem(z + 4 - dz, 4) + k
            part = jnp.zeros((16, 512), F32)
            for h in range(2):
                rows = jnp.concatenate([si[e * 2 + h, g, 0:16, :], si[e * 2 + h, g, 16:32, :]], axis=1)
                at = pl.multiple_of(h * 512 + g * 256, 256)
                part = part + jnp.dot(rows, win[e, pl.ds(at, 256), :], preferred_element_type=F32)
            parts.append(part)
        return jnp.concatenate(parts, axis=0)

    xp = []
    for dz in GROUPS:
        arrive(dz)
        ld_win[dz].wait()
        h_half[dz] = half(dz, c)
    for dz in GROUPS:
        whole(dz)
        q = lax.rem(z + 4 - dz, 4)
        d = lax.rem(q + 4 - x, 4)
        own = h_half[dz] + half(dz, 1 - c)
        hp[dz] = own.astype(BF16)
        xp.append(remote_if(d != 0, hp.at[dz], hr.at[d], x_send.at[3, dz], x_recv.at[3, d], (s, q)))

        @pl.when(d == 0)
        def _(own=own):
            h_own[...] = own

    drain(count)
    xh = {d: arrival(hr.at[d], x_send.at[3, 0], x_recv.at[3, d]) for d in (1, 2, 3)}
    via_a.wait_recv()
    nsend[1, 0:128, :] = nsend[1, 0:128, :] + relay_a[...]
    via_b.wait_recv()
    nsend[3, 128:256, :] = nsend[3, 128:256, :] + relay_b[...]
    sent(xp)
    piece(1, 0, 24, 9)
    piece(3, 128, 24, 9)
    hidden = h_own[...]
    for d in (1, 3, 2):
        xh[d].wait_recv()
        hidden = hidden + hr[d].astype(F32)
    hidden = 0.5 * hidden * (1.0 + lax.erf(hidden * 0.7071067811865476))
    hb[x] = hidden.astype(BF16)
    xg = {d: remote(hb.at[x], hb.at[x], x_send.at[4, d], x_recv.at[4, d], xdev(d)) for d in SENDS}

    drain(len(pending) - 3)
    sent(list(xg.values()))
    piece(1, 24, 104, 10)
    piece(3, 152, 104, 10)
    piece(1, 240, 16, 12)
    piece(3, 112, 16, 12)
    def chips_sum(q, copy):
        copy.wait_recv()
        block = pl.ds(4 * q, 4)
        ab2[block] = (ob[c, block] + po[block]).astype(BF16)
        dz = lax.rem(q + 4 - z, 4)
        for dy in range(4):
            to = q * 4 + lax.rem(y + dy, 4)
            j = dz * 4 + dy
            args = (ab2.at[to], ro.at[j], s_send.at[2, j], s_recv.at[2, j], (to * 2 + c, x))
            if dy:
                remote(*args)
            else:
                remote_if(dz != 0, *args)

    count = len(pending)
    last = None
    for i, d in enumerate(ARRIVALS):
        q = lax.rem(x + 4 - d, 4)
        if d:
            xg[d].wait_recv()
        ld_wout[d].wait()
        for k in range(2):
            e = 2 * q + k
            o = jnp.dot(hb[q, k * 16:(k + 1) * 16, :], wout[e], preferred_element_type=F32)
            for h in range(2):
                for g in range(2):
                    for b in range(2):
                        at = h * 512 + g * 256 + b * 128
                        ob[g, e * 2 + h, b * 16:(b + 1) * 16, :] = o[:, at:at + 128]
        block = pl.ds(4 * q, 4)
        copy = remote(ob.at[1 - c, block], po.at[block], c_send.at[1 + i], c_recv.at[1 + i], peer)
        if last is not None:
            chips_sum(*last)
        last = (q, copy)
    chips_sum(*last)
    drain(count)
    sv = {j: arrival(ro.at[j], s_send.at[2, 0], s_recv.at[2, j]) for j in range(1, CHIPS)}
    for j in range(1, CHIPS):
        sv[j].wait_recv()
    acc = ab2[p].astype(F32)
    for j in range(1, CHIPS):
        acc = acc + ro[j].astype(F32)
    so[p, c, :, :] = acc.astype(BF16)
    count = len(pending)
    arrive, whole = gather(so, 3)
    drain(count)

    for cp in xn:
        cp.wait_recv()
    for d in SENDS:
        xq[d].wait_recv()
    cnn = jnp.sqrt(cq[0] + cq[1] + cq[2] + cq[3] + EPS)
    for g in range(4):
        r = slice(g * 64, (g + 1) * 64)
        rg = rnv[r, :]
        lwin = lw[r, :]
        ls = []
        top = lwin
        for b in range(7):
            at = slice(b * 128, (b + 1) * 128)
            raw = nsend[0, r, at] + nrecv[0, r, at] + nrecv[1, r, at]
            lg = scale * raw / (rg * cnn[b:b + 1])
            ls.append(lg)
            top = jnp.maximum(top, lg)
        tmax = jnp.max(top, axis=1, keepdims=True)
        ew = jnp.exp(lwin - tmax)
        tsum = ew
        for lg in ls:
            tsum = tsum + jnp.exp(lg - tmax)
        ttot = jnp.sum(tsum, axis=1, keepdims=True)
        cb[x, r, :] = (ew / ttot).astype(BF16)
    xc = {d: remote(cb.at[x], cb.at[x], x_send.at[5, d], x_recv.at[5, d], xdev(d)) for d in SENDS}

    for dz in GROUPS:
        arrive(dz)
    for d in SENDS:
        xc[d].wait_recv()
    store_comb = load(cb, comb_o, 14)
    for dz in GROUPS:
        whole(dz)
    load(so, so_o, 15).wait()
    store_comb.wait()
    for cond, cp in pending + bulk:
        if cond is None:
            cp.wait_send()
        else:
            pl.when(cond)(cp.wait_send)


def mix(comb, so, out_h, slot_out, out, sem):
    def copy(src, dst, i):
        cp = pltpu.make_async_copy(src, dst, sem.at[i])
        cp.start()
        return cp

    for e in range(E_RUN):
        for h in range(2):
            for g in range(2):
                for b in range(2):
                    at = h * 512 + g * 256 + b * 128
                    slot_out[e * 16:(e + 1) * 16, at:at + 128] = so[e * 2 + h, g, b * 16:(b + 1) * 16, :]
    stores = []
    for g in range(4):
        r = pl.ds(g * QT, QT)
        out[r, :] = jnp.dot(comb[g], slot_out[...], preferred_element_type=F32).astype(BF16)
        stores.append(copy(out.at[r], out_h.at[r], g))
    for cp in stores:
        cp.wait()


def per_device(tokens, slot_param, scale, w_in, w_out):
    vm = pltpu.VMEM
    dma = pltpu.SemaphoreType.DMA
    anyspec = pl.BlockSpec(memory_space=pl.ANY)
    comb, slot_out = pl.pallas_call(
        kernel,
        name="moe_exchange",
        out_shape=(jax.ShapeDtypeStruct((4, QT, 128), BF16), jax.ShapeDtypeStruct((16, 2, 32, 128), BF16)),
        in_specs=[anyspec, anyspec, anyspec, anyspec, anyspec],
        out_specs=(anyspec, anyspec),
        scratch_shapes=[
            pltpu.SMEM((1,), F32), vm((1024, 1024), BF16), vm((1024, 128), BF16), vm((1024, REST), BF16),
            vm((8, 1024, 512), BF16), vm((8, 512, 1024), BF16),
            vm((4, QT + 8, 128), F32), vm((4, QT + 8, 128), F32), vm((QT, 128), F32), vm((QT, 128), F32),
            vm((4, QT + 16, 128), BF16),
            vm((4, 8, 128), F32), vm((4, QT, REST), F32), vm((2, QT, REST), F32), vm((128, REST), F32), vm((128, REST), F32),
            vm((2, 16, 40, 128), F32), vm((2, 128, 128), F32), vm((16, 40, 128), F32), vm((16, 48, 128), BF16), vm((16, 48, 128), BF16),
            vm((128, 128), F32), vm((16, 2, 32, 128), BF16),
            vm((4, 32, 512), BF16), vm((4, 32, 512), BF16), vm((32, 512), F32), vm((4, 32, 512), F32), vm((4, 32, 512), BF16),
            vm((2, 16, 32, 128), F32), vm((16, 32, 128), F32), vm((16, 32, 128), BF16), vm((16, 32, 128), BF16),
            vm((16, 2, 32, 128), BF16), vm((4, QT, 128), BF16),
            pltpu.SemaphoreType.REGULAR, dma((17,)), dma((13, 4)), dma((13, 4)), dma((5,)), dma((5,)),
            dma((4, 16)), dma((4, 16)), dma((4, 16)), dma((4, 16)),
        ],
        compiler_params=pltpu.CompilerParams(
            collective_id=0, has_side_effects=True, vmem_limit_bytes=53 * 2**20
        ),
    )(tokens, slot_param, scale, w_in, w_out)
    return pl.pallas_call(
        mix,
        name="mix",
        out_shape=jax.ShapeDtypeStruct((1024, 1024), BF16),
        in_specs=[pl.BlockSpec(memory_space=pltpu.VMEM)] * 2,
        out_specs=anyspec,
        scratch_shapes=[vm((128, 1024), BF16), vm((1024, 1024), BF16), dma((4,))],
        compiler_params=pltpu.CompilerParams(vmem_limit_bytes=16 * 2**20),
    )(comb, slot_out)


def solution(mesh):
    in_specs = (
        P("seq", "width"),
        P("width", None),
        P(),
        P(None, "width", "seq"),
        P(None, "seq", "width"),
    )
    return jax.shard_map(
        per_device, mesh=mesh, in_specs=in_specs, out_specs=P("seq", "width"), check_vma=False
    )
```

```python
import jax
import jax.numpy as jnp
from jax import lax
from jax.experimental import pallas as pl
from jax.experimental.pallas import tpu as pltpu
from jax.sharding import PartitionSpec as P

SLOT_PER = 16
E_RUN = 8
WINDOW = 128
EPS = 1e-06
F32 = jnp.float32
BF16 = jnp.bfloat16
MESH = pl.DeviceIdType.MESH
QT = 256
REST = 896
CHIPS = 16
SENDS = (2, 1, 3)
ARRIVALS = (0, 1, 3, 2)
GROUPS = (0, 1, 3, 2)


def hops(j):
    return (0, 1, 2, 1)[j // 4] + (0, 1, 2, 1)[j % 4]


AXIS = (8, 2, 4, 12, 1, 3)
OTHERS = sorted(range(1, CHIPS), key=lambda j: -hops(j))


def column(row):
    return jnp.transpose(jnp.broadcast_to(row, (128, 128)))


def kernel(
    tok_h, sp_h, scale_h, win_h, wout_h,
    comb_o, so_o,
    scale_ref, tok, spw, spn, win, wout,
    wsend, wrecv, lw, rnv, dsp, cq, nsend, nrecv, relay_a, relay_b,
    wb, fs, pr, ab, rb, gs, si,
    hp, hr, h_own, h_half, hb, ob, po, ab2, ro, so, cb,
    ready, ld_sem, x_send, x_recv, c_send, c_recv, s_send, s_recv, f_send, f_recv,
):
    s = lax.axis_index("seq")
    x = lax.axis_index("width")
    c = lax.rem(s, 2)
    p = lax.div(s, 2)
    z = lax.div(p, 4)
    y = lax.rem(p, 4)
    peer = (s + 1 - 2 * c, x)

    def xdev(d):
        return (s, lax.rem(x + d, 4))

    def chip_of(j):
        return lax.rem(z + j // 4, 4) * 4 + lax.rem(y + j % 4, 4)

    def chip_from(j):
        return lax.rem(z + 4 - j // 4, 4) * 4 + lax.rem(y + 4 - j % 4, 4)

    pending, bulk = [], []

    def remote(src, dst, send, recv, to):
        cp = pltpu.make_async_remote_copy(
            src_ref=src, dst_ref=dst, send_sem=send, recv_sem=recv, device_id=to, device_id_type=MESH
        )
        cp.start()
        pending.append((None, cp))
        return cp

    def remote_if(cond, src, dst, send, recv, to):
        cp = pltpu.make_async_remote_copy(
            src_ref=src, dst_ref=dst, send_sem=send, recv_sem=recv, device_id=to, device_id_type=MESH
        )
        pl.when(cond)(cp.start)
        pending.append((cond, cp))
        return cp

    def sent(copies):
        for cp in copies:
            for k, (cond, other) in enumerate(pending):
                if other is cp:
                    del pending[k]
                    break
            if cond is None:
                cp.wait_send()
            else:
                pl.when(cond)(cp.wait_send)

    def drain(count):
        for cond, cp in pending[:count]:
            if cond is None:
                cp.wait_send()
            else:
                pl.when(cond)(cp.wait_send)
        del pending[:count]

    xn = []

    def piece(d, start, count, k):
        rows, slot = pl.ds(start, count), d // 2
        xn.append(remote(nsend.at[d, rows], nrecv.at[slot, rows], x_send.at[k, slot], x_recv.at[k, slot], xdev(d)))
        bulk.append(pending.pop())

    def arrival(dst, send, recv):
        return pltpu.make_async_remote_copy(
            src_ref=dst, dst_ref=dst, send_sem=send, recv_sem=recv, device_id=peer, device_id_type=MESH
        )

    barrier = pltpu.get_barrier_semaphore()
    for j in AXIS:
        pl.semaphore_signal(barrier, inc=1, device_id=(chip_of(j) * 2 + c, x), device_id_type=MESH)
    for d in SENDS:
        pl.semaphore_signal(barrier, inc=1, device_id=xdev(d), device_id_type=MESH)
    pl.semaphore_signal(barrier, inc=1, device_id=peer, device_id_type=MESH)

    def load(src, dst, i):
        cp = pltpu.make_async_copy(src, dst, ld_sem.at[i])
        cp.start()
        return cp

    ld_scale = load(scale_h, scale_ref, 16)
    ld_spw = load(sp_h.at[:, pl.ds(0, WINDOW)], spw, 0)
    ld_tok = {}
    for i, d in enumerate((2, 1, 3, 0)):
        rows = pl.ds(lax.rem(x + d, 4) * QT, QT)
        ld_tok[d] = load(tok_h.at[rows], tok.at[rows], 1 + i)
    ld_spn = load(sp_h.at[:, pl.ds(WINDOW, REST)], spn, 5)
    ld_spw.wait()
    spf = spw[...].astype(F32)
    csq = jnp.sum(spf * spf, axis=0, keepdims=True)
    xw = {}
    for d in (2, 1, 3, 0):
        ld_tok[d].wait()
        t = tok[pl.ds(lax.rem(x + d, 4) * QT, QT), :]
        wsend[d, 0:QT, :] = jnp.dot(t, spw[...], preferred_element_type=F32)
        part = jnp.zeros((QT, 128), F32)
        for b in range(8):
            tf = t[:, b * 128:(b + 1) * 128].astype(F32)
            part = part + tf * tf
        rows = [jnp.sum(jnp.transpose(part[h * 128:(h + 1) * 128]), axis=0, keepdims=True) for h in range(2)]
        wsend[d, QT:QT + 8, :] = jnp.concatenate(rows + [csq, jnp.zeros((5, 128), F32)], axis=0)
        if d == 2:
            pl.semaphore_wait(barrier, 4 + len(AXIS))
        if d:
            xw[d] = remote(wsend.at[d], wrecv.at[d], x_send.at[0, d], x_recv.at[0, d], xdev(d))
    for j in (8, 4, 12):
        pl.semaphore_signal(ready, inc=1, device_id=(chip_of(j) * 2 + c, x), device_id_type=MESH)

    ld_win = {}
    for i, dz in enumerate(GROUPS):
        e = 2 * lax.rem(z + 4 - dz, 4)
        ld_win[dz] = load(win_h.at[pl.ds(e, 2)], win.at[pl.ds(e, 2)], 6 + i)
    ld_wout = {}
    for i, d in enumerate(ARRIVALS):
        e = 2 * lax.rem(x + 4 - d, 4)
        ld_wout[d] = load(wout_h.at[pl.ds(e, 2)], wout.at[pl.ds(e, 2)], 10 + i)

    ld_spn.wait()
    csn = jnp.zeros((8, REST), F32)
    for b in range(32):
        sf = spn[b * 32:(b + 1) * 32, :].astype(F32)
        sq = sf * sf
        csn = csn + sq[0:8] + sq[8:16] + sq[16:24] + sq[24:32]
    csr = jnp.sum(csn, axis=0, keepdims=True)
    cq[0] = jnp.concatenate([csr[:, b * 128:(b + 1) * 128] for b in range(7)] + [jnp.ones((1, 128), F32)], axis=0)
    xq = {d: remote(cq.at[0], cq.at[d], x_send.at[11, d], x_recv.at[11, d], xdev(d)) for d in SENDS}
    for d in (2, 1, 3, 0):
        t = tok[pl.ds(lax.rem(x + d, 4) * QT, QT), :]
        nsend[d, 0:QT, :] = jnp.dot(t, spn[...], preferred_element_type=F32)

    sent(list(xw.values()))
    piece(1, 128, 40, 6)
    piece(3, 0, 40, 6)
    tot = wsend[0]
    for d in (1, 3, 2):
        xw[d].wait_recv()
        tot = tot + wrecv[d]
    rn = jnp.sqrt(jnp.concatenate([column(tot[QT:QT + 1]), column(tot[QT + 1:QT + 2])], axis=0) + EPS)
    cn = jnp.sqrt(tot[QT + 2:QT + 3] + EPS)
    ld_scale.wait()
    scale = scale_ref[0]
    logits = scale * tot[0:QT] / (rn * cn)
    lw[...] = logits
    rnv[...] = rn
    m = jnp.max(logits, axis=0, keepdims=True).astype(BF16)
    dsp[x, 0:QT, :] = jnp.exp(logits - m.astype(F32)).astype(BF16)
    dsp[x, QT:QT + 16, :] = jnp.broadcast_to(m, (16, 128))
    xd = {d: remote(dsp.at[x], dsp.at[x], x_send.at[1, d], x_recv.at[1, d], xdev(d)) for d in SENDS}

    sent(list(xd.values()))
    piece(1, 168, 40, 7)
    piece(3, 40, 40, 7)
    for d in SENDS:
        xd[d].wait_recv()
    via_a = remote(nsend.at[2, pl.ds(0, 128)], relay_a, x_send.at[2, 0], x_recv.at[2, 0], xdev(1))
    via_b = remote(nsend.at[2, pl.ds(128, 128)], relay_b, x_send.at[2, 1], x_recv.at[2, 1], xdev(3))
    bulk.extend((pending.pop(), pending.pop()))
    ms = [dsp[q, QT:QT + 1, :].astype(F32) for q in range(4)]
    mseq = jnp.maximum(jnp.maximum(ms[0], ms[1]), jnp.maximum(ms[2], ms[3]))
    total = jnp.zeros((1, 128), F32)
    cols = []
    for q in range(4):
        f = jnp.exp(ms[q] - mseq)
        total = total + f * jnp.sum(dsp[q, 0:QT, :].astype(F32), axis=0, keepdims=True)
        cols.append(column(f))
    stats = jnp.concatenate([mseq, total, jnp.zeros((6, 128), F32)], axis=0)
    cw = None
    for k in (1 - c, c):
        for h in range(2):
            at = pl.multiple_of(h * 512 + k * 256, 256)
            acc = jnp.zeros((128, 256), F32)
            for q in range(4):
                prod = lax.dot_general(
                    dsp[q, 0:QT, :], tok[q * QT:(q + 1) * QT, pl.ds(at, 256)],
                    (((0,), (0,)), ((), ())), preferred_element_type=F32,
                )
                acc = acc + prod * jnp.concatenate([cols[q], cols[q]], axis=1)
            for e in range(E_RUN):
                for b in range(2):
                    wb[k, e * 2 + h, b * 16:(b + 1) * 16, :] = acc[e * 16:(e + 1) * 16, b * 128:(b + 1) * 128]
                wb[k, e * 2 + h, 32:40, :] = stats
        if cw is None:
            cw = remote(wb.at[1 - c], pr, c_send.at[0], c_recv.at[0], peer)

    cw.wait_recv()
    m_a, m_b = wb[c, 0, 32:33, :], pr[0, 32:33, :]
    m2 = jnp.maximum(m_a, m_b)
    f_a, f_b = jnp.exp(m_a - m2), jnp.exp(m_b - m2)
    t2 = f_a * wb[c, 0, 33:34, :] + f_b * pr[0, 33:34, :]
    t_hi = t2.astype(BF16).astype(F32)
    stats = jnp.concatenate([m2, t_hi, t2 - t_hi, jnp.zeros((13, 128), F32)], axis=0).astype(BF16)
    fs[0], fs[1] = column(f_a), column(f_b)
    pl.semaphore_wait(ready, 3)
    sw = {}
    for j in OTHERS + [0]:
        i = chip_of(j)
        rows = pl.ds(lax.div(i, 2) * 16, 16)
        k_a, k_b = fs[0, rows, :], fs[1, rows, :]
        for b in range(2):
            r = slice(b * 16, (b + 1) * 16)
            ab[i, r, :] = (wb[c, i, r, :] * k_a + pr[i, r, :] * k_b).astype(BF16)
        ab[i, 32:48, :] = stats
        if j:
            sw[j] = remote(ab.at[i], rb.at[j], s_send.at[0, j], s_recv.at[0, j], (i * 2 + c, x))
    drain(len(pending) - 15)
    for j in range(1, CHIPS):
        sw[j].wait_recv()
    piece(1, 208, 32, 8)
    piece(3, 80, 32, 8)
    st = [ab[p, 32:48, :].astype(F32)] + [rb[j, 32:48, :].astype(F32) for j in range(1, CHIPS)]
    mr = [v[0:1] for v in st]
    tr = [v[1:2] + v[2:3] for v in st]
    top = mr[0]
    for v in mr[1:]:
        top = jnp.maximum(top, v)
    fr = [jnp.exp(v - top) for v in mr]
    total = fr[0] * tr[0]
    for f, t in zip(fr[1:], tr[1:]):
        total = total + f * t
    gs[...] = jnp.transpose(jnp.concatenate([f / total for f in fr] + [jnp.zeros((112, 128), F32)], axis=0))
    ge = gs[pl.ds(lax.div(p, 2) * 16, 16), :]
    acc = [jnp.zeros((16, 128), F32)] * 2
    for j in range(CHIPS):
        w = ge[:, j:j + 1]
        for b in range(2):
            r = slice(b * 16, (b + 1) * 16)
            v = ab[p, r, :] if j == 0 else rb[j, r, :]
            acc[b] = acc[b] + v.astype(F32) * w
    si[p, c, :, :] = jnp.concatenate(acc, axis=0).astype(BF16)


    def gather(buf, k):
        out, other = {}, {}
        for j in OTHERS:
            to = (chip_of(j) * 2 + c, x)
            out[j] = remote(buf.at[p, c], buf.at[p, c], s_send.at[k, j], s_recv.at[k, j], to)
        other[0] = remote(buf.at[p, c], buf.at[p, c], f_send.at[k, 0], f_recv.at[k, 0], peer)

        def arrive(dz):
            for j in range(dz * 4, dz * 4 + 4):
                if j:
                    out[j].wait_recv()
                    at = chip_from(j)
                    other[j] = remote(buf.at[at, c], buf.at[at, c], f_send.at[k, j], f_recv.at[k, j], peer)

        def whole(dz):
            for j in range(dz * 4, dz * 4 + 4):
                other[j].wait_recv()

        return arrive, whole

    count = len(pending)
    arrive, whole = gather(si, 1)
    drain(count)
    count = len(pending)

    def half(dz, g):
        parts = []
        for k in range(2):
            e = 2 * lax.rem(z + 4 - dz, 4) + k
            part = jnp.zeros((16, 512), F32)
            for h in range(2):
                rows = jnp.concatenate([si[e * 2 + h, g, 0:16, :], si[e * 2 + h, g, 16:32, :]], axis=1)
                at = pl.multiple_of(h * 512 + g * 256, 256)
                part = part + jnp.dot(rows, win[e, pl.ds(at, 256), :], preferred_element_type=F32)
            parts.append(part)
        return jnp.concatenate(parts, axis=0)

    xp = []
    for dz in GROUPS:
        arrive(dz)
        ld_win[dz].wait()
        h_half[dz] = half(dz, c)
    for dz in GROUPS:
        whole(dz)
        q = lax.rem(z + 4 - dz, 4)
        d = lax.rem(q + 4 - x, 4)
        own = h_half[dz] + half(dz, 1 - c)
        hp[dz] = own.astype(BF16)
        xp.append(remote_if(d != 0, hp.at[dz], hr.at[d], x_send.at[3, dz], x_recv.at[3, d], (s, q)))

        @pl.when(d == 0)
        def _(own=own):
            h_own[...] = own

    drain(count)
    xh = {d: arrival(hr.at[d], x_send.at[3, 0], x_recv.at[3, d]) for d in (1, 2, 3)}
    via_a.wait_recv()
    nsend[1, 0:128, :] = nsend[1, 0:128, :] + relay_a[...]
    via_b.wait_recv()
    nsend[3, 128:256, :] = nsend[3, 128:256, :] + relay_b[...]
    sent(xp)
    piece(1, 0, 24, 9)
    piece(3, 128, 24, 9)
    hidden = h_own[...]
    for d in (1, 3, 2):
        xh[d].wait_recv()
        hidden = hidden + hr[d].astype(F32)
    hidden = 0.5 * hidden * (1.0 + lax.erf(hidden * 0.7071067811865476))
    hb[x] = hidden.astype(BF16)
    xg = {d: remote(hb.at[x], hb.at[x], x_send.at[4, d], x_recv.at[4, d], xdev(d)) for d in SENDS}

    drain(len(pending) - 3)
    sent(list(xg.values()))
    piece(1, 24, 104, 10)
    piece(3, 152, 104, 10)
    piece(1, 240, 16, 12)
    piece(3, 112, 16, 12)
    def chips_sum(q, copy):
        copy.wait_recv()
        block = pl.ds(4 * q, 4)
        ab2[block] = (ob[c, block] + po[block]).astype(BF16)
        dz = lax.rem(q + 4 - z, 4)
        for dy in range(4):
            to = q * 4 + lax.rem(y + dy, 4)
            j = dz * 4 + dy
            args = (ab2.at[to], ro.at[j], s_send.at[2, j], s_recv.at[2, j], (to * 2 + c, x))
            if dy:
                remote(*args)
            else:
                remote_if(dz != 0, *args)

    count = len(pending)
    last = None
    for i, d in enumerate(ARRIVALS):
        q = lax.rem(x + 4 - d, 4)
        if d:
            xg[d].wait_recv()
        ld_wout[d].wait()
        for k in range(2):
            e = 2 * q + k
            o = jnp.dot(hb[q, k * 16:(k + 1) * 16, :], wout[e], preferred_element_type=F32)
            for h in range(2):
                for g in range(2):
                    for b in range(2):
                        at = h * 512 + g * 256 + b * 128
                        ob[g, e * 2 + h, b * 16:(b + 1) * 16, :] = o[:, at:at + 128]
        block = pl.ds(4 * q, 4)
        copy = remote(ob.at[1 - c, block], po.at[block], c_send.at[1 + i], c_recv.at[1 + i], peer)
        if last is not None:
            chips_sum(*last)
        last = (q, copy)
    chips_sum(*last)
    drain(count)
    sv = {j: arrival(ro.at[j], s_send.at[2, 0], s_recv.at[2, j]) for j in range(1, CHIPS)}
    for j in range(1, CHIPS):
        sv[j].wait_recv()
    acc = ab2[p].astype(F32)
    for j in range(1, CHIPS):
        acc = acc + ro[j].astype(F32)
    so[p, c, :, :] = acc.astype(BF16)
    count = len(pending)
    arrive, whole = gather(so, 3)
    drain(count)

    for cp in xn:
        cp.wait_recv()
    for d in SENDS:
        xq[d].wait_recv()
    cnn = jnp.sqrt(cq[0] + cq[1] + cq[2] + cq[3] + EPS)
    for g in range(4):
        r = slice(g * 64, (g + 1) * 64)
        rg = rnv[r, :]
        lwin = lw[r, :]
        ls = []
        top = lwin
        for b in range(7):
            at = slice(b * 128, (b + 1) * 128)
            raw = nsend[0, r, at] + nrecv[0, r, at] + nrecv[1, r, at]
            lg = scale * raw / (rg * cnn[b:b + 1])
            ls.append(lg)
            top = jnp.maximum(top, lg)
        tmax = jnp.max(top, axis=1, keepdims=True)
        ew = jnp.exp(lwin - tmax)
        tsum = ew
        for lg in ls:
            tsum = tsum + jnp.exp(lg - tmax)
        ttot = jnp.sum(tsum, axis=1, keepdims=True)
        cb[x, r, :] = (ew / ttot).astype(BF16)
    xc = {d: remote(cb.at[x], cb.at[x], x_send.at[5, d], x_recv.at[5, d], xdev(d)) for d in SENDS}

    for dz in GROUPS:
        arrive(dz)
    for d in SENDS:
        xc[d].wait_recv()
    store_comb = load(cb, comb_o, 14)
    for dz in GROUPS:
        whole(dz)
    load(so, so_o, 15).wait()
    store_comb.wait()
    for cond, cp in pending + bulk:
        if cond is None:
            cp.wait_send()
        else:
            pl.when(cond)(cp.wait_send)


def mix(comb, so, out_h, slot_out, out, sem):
    def copy(src, dst, i):
        cp = pltpu.make_async_copy(src, dst, sem.at[i])
        cp.start()
        return cp

    for e in range(E_RUN):
        for h in range(2):
            for g in range(2):
                for b in range(2):
                    at = h * 512 + g * 256 + b * 128
                    slot_out[e * 16:(e + 1) * 16, at:at + 128] = so[e * 2 + h, g, b * 16:(b + 1) * 16, :]
    stores = []
    for g in range(8):
        r = pl.ds(g * 128, 128)
        out[r, :] = jnp.dot(comb[g // 2, g % 2 * 128:g % 2 * 128 + 128, :], slot_out[...], preferred_element_type=F32).astype(BF16)
        stores.append(copy(out.at[r], out_h.at[r], g))
    for cp in stores:
        cp.wait()


def per_device(tokens, slot_param, scale, w_in, w_out):
    vm = pltpu.VMEM
    dma = pltpu.SemaphoreType.DMA
    anyspec = pl.BlockSpec(memory_space=pl.ANY)
    comb, slot_out = pl.pallas_call(
        kernel,
        name="moe_exchange",
        out_shape=(jax.ShapeDtypeStruct((4, QT, 128), BF16), jax.ShapeDtypeStruct((16, 2, 32, 128), BF16)),
        in_specs=[anyspec, anyspec, anyspec, anyspec, anyspec],
        out_specs=(anyspec, anyspec),
        scratch_shapes=[
            pltpu.SMEM((1,), F32), vm((1024, 1024), BF16), vm((1024, 128), BF16), vm((1024, REST), BF16),
            vm((8, 1024, 512), BF16), vm((8, 512, 1024), BF16),
            vm((4, QT + 8, 128), F32), vm((4, QT + 8, 128), F32), vm((QT, 128), F32), vm((QT, 128), F32),
            vm((4, QT + 16, 128), BF16),
            vm((4, 8, 128), F32), vm((4, QT, REST), F32), vm((2, QT, REST), F32), vm((128, REST), F32), vm((128, REST), F32),
            vm((2, 16, 40, 128), F32), vm((2, 128, 128), F32), vm((16, 40, 128), F32), vm((16, 48, 128), BF16), vm((16, 48, 128), BF16),
            vm((128, 128), F32), vm((16, 2, 32, 128), BF16),
            vm((4, 32, 512), BF16), vm((4, 32, 512), BF16), vm((32, 512), F32), vm((4, 32, 512), F32), vm((4, 32, 512), BF16),
            vm((2, 16, 32, 128), F32), vm((16, 32, 128), F32), vm((16, 32, 128), BF16), vm((16, 32, 128), BF16),
            vm((16, 2, 32, 128), BF16), vm((4, QT, 128), BF16),
            pltpu.SemaphoreType.REGULAR, dma((17,)), dma((13, 4)), dma((13, 4)), dma((5,)), dma((5,)),
            dma((4, 16)), dma((4, 16)), dma((4, 16)), dma((4, 16)),
        ],
        compiler_params=pltpu.CompilerParams(
            collective_id=0, has_side_effects=True, vmem_limit_bytes=53 * 2**20
        ),
    )(tokens, slot_param, scale, w_in, w_out)
    return pl.pallas_call(
        mix,
        name="mix",
        out_shape=jax.ShapeDtypeStruct((1024, 1024), BF16),
        in_specs=[pl.BlockSpec(memory_space=pltpu.VMEM)] * 2,
        out_specs=anyspec,
        scratch_shapes=[vm((128, 1024), BF16), vm((1024, 1024), BF16), dma((8,))],
        compiler_params=pltpu.CompilerParams(vmem_limit_bytes=16 * 2**20),
    )(comb, slot_out)


def solution(mesh):
    in_specs = (
        P("seq", "width"),
        P("width", None),
        P(),
        P(None, "width", "seq"),
        P(None, "seq", "width"),
    )
    return jax.shard_map(
        per_device, mesh=mesh, in_specs=in_specs, out_specs=P("seq", "width"), check_vma=False
    )
```
